128 devices in a mesh: graph: 128 (over y, x, z, core).
Axes of the slice: x: 4, y: 4, z: 4, core: 2. Of those that a mesh axis runs over, the one named last changes fastest.
Arguments:
- node_coef: bfloat16 [8192, 29, 128], P('graph'), may hold values from -6 to 6
- cotangent: bfloat16 [8192, 29, 128], P('graph'), may hold values from -6 to 6
- wigner: bfloat16 [64, 29, 29], replicated, as said below
- envelope: float32 [1536, 64], P('graph'), may hold values from 0.2 to 1
- src_tile: int32 [1536], P('graph'), may hold values from 0 to 127, as said below
- dst_tile: int32 [1536], P('graph'), may hold values from 0 to 127, as said below
- src_slot: int32 [1536, 64], P('graph'), may hold values from 0 to 63
- dst_slot: int32 [1536, 64], P('graph'), may hold values from 0 to 63
- bucket: int32 [1536, 64], P('graph'), may hold values from 0 to 63
- mask: int32 [1536, 64], P('graph'), may hold values from 0 to 1, as said below
- w_zero: bfloat16 [896, 896], replicated, may hold values from -0.1875 to 0.1875
- w_one: bfloat16 [2, 768, 768], replicated, may hold values from -0.15625 to 0.15625
- w_two: bfloat16 [2, 640, 640], replicated, may hold values from -0.15625 to 0.15625
Outputs:
- updated: bfloat16 [8192, 29, 128], P('graph')
- grad_coef: bfloat16 [8192, 29, 128], P('graph')
- grad_zero: float32 [802816], P('graph')
- grad_one: float32 [1179648], P('graph')
- grad_two: float32 [819200], P('graph')
The draws below stay inside these ranges and needn't reach their ends.
Inputs may be any that keep to these rules, and one draw needn't show every extreme that they name: Block b's source tile lies on the device b // 12 or one beside it: src_tile // 1 differs from b // 12 by at most 1. Block b's destination tile lies on the device b // 12 or one beside it: dst_tile // 1 differs from b // 12 by at most 1. `mask`: at least 6 blocks of each owner hold live edges. `wigner`: entry (i, j) is zero unless coefficients i and j have the same degree.
All inputs are finite; a program needn't handle non-finite values.
Results may differ from the reference program's by a relative error of at most 0.0053.
Values may be sent and summed in bfloat16 or wider, within the bound.
No kernel may reach another device: no remote copies, remote signals or barrier semaphores. Data moves between devices by JAX's collectives and lax.ppermute only.
A program may use at most 192 MiB of HBM per device.

```python
import math
import jax
import jax.numpy as jnp
import numpy as np
from jax import lax

C = 128
NCOEF = 29
TILE = 64
EB = 64
BUCKETS = 64
TILES_DEV = 1
BLK_DEV = 12
ATOMS = 8192
TILES = 128
BLOCKS = 1536
N_GRAPH = 128


def tile_draw(key):
    owner = jnp.arange(BLOCKS, dtype=jnp.int32) // BLK_DEV
    devices = BLOCKS // BLK_DEV
    offset = jax.random.randint(jax.random.fold_in(key, 1), (BLOCKS,), -1, 2, dtype=jnp.int32)
    device = jnp.clip(owner + offset, 0, devices - 1)
    within = jax.random.randint(jax.random.fold_in(key, 2), (BLOCKS,), 0, TILES_DEV, dtype=jnp.int32)
    tiles = device * TILES_DEV + within
    tiles = tiles.at[0].set(0)
    tiles = tiles.at[BLOCKS - 1].set(TILES - 1)
    return tiles.astype(jnp.int32)


def draw_src_tile(key, part):
    key = jax.random.fold_in(key, 5)
    return tile_draw(key)


def draw_dst_tile(key, part):
    key = jax.random.fold_in(key, 6)
    return tile_draw(key)


def draw_mask(key, part):
    key = jax.random.fold_in(key, 7)
    owners = BLOCKS // BLK_DEV
    live_count = jax.random.randint(jax.random.fold_in(key, 1), (owners,), BLK_DEV // 2, BLK_DEV + 1, dtype=jnp.int32)
    live_count = live_count.at[0].set(BLK_DEV)
    position = jnp.arange(BLOCKS, dtype=jnp.int32) % BLK_DEV
    owner = jnp.arange(BLOCKS, dtype=jnp.int32) // BLK_DEV
    live_block = position < live_count[owner]
    dense = jax.random.randint(jax.random.fold_in(key, 2), (BLOCKS, EB), 0, 8, dtype=jnp.int32) < 7
    dense = dense.at[:, 0].set(True)
    return jnp.where(live_block[:, None] & dense, 1, 0).astype(jnp.int32)


def draw_wigner(key, part):
    key = jax.random.fold_in(key, 11)
    degree = np.array([0, 1, 2, 3, 4, 5, 6, 1, 2, 3, 4, 5, 6, 1, 2, 3, 4, 5, 6, 2, 3, 4, 5, 6, 2, 3, 4, 5, 6])
    same = jnp.asarray(degree[:, None] == degree[None, :])
    widths = np.minimum(degree, 2) * 2 + 1
    factor = jnp.asarray(1.0 / np.sqrt(widths), dtype=jnp.float32)
    values = jax.random.normal(key, (BUCKETS, NCOEF, NCOEF), jnp.float32)
    table = jnp.where(same[None], values * factor[None, :, None], 0.0)
    table = table.at[:, 0, 0].set(1.0)
    return table.astype(jnp.bfloat16)


def with_ends(result, own_key, least, top_value):
    index_at = [jax.random.randint(jax.random.fold_in(own_key, axis), (), 0, length) for axis, length in enumerate(result.shape)]
    longest = result.shape.index(max(result.shape))
    beside = index_at[:longest] + [(index_at[longest] + 1) % result.shape[longest]] + index_at[longest + 1:]
    return result.at[tuple(index_at)].set(least).at[tuple(beside)].set(top_value)


def level_of(stream_key, shape, shards, smallest, largest):
    def one(dim, blocks):
        heights = jax.random.uniform(jax.random.fold_in(jax.random.fold_in(stream_key, 6), dim), (blocks,), jnp.float32, smallest / len(shards), largest / len(shards))
        return jnp.repeat(jnp.exp(heights), shape[dim] // blocks).reshape((-1,) + (1,) * (len(shape) - dim - 1))

    factor_of = one(*shards[0])
    for cut in shards[1:]:
        factor_of = factor_of * one(*cut)
    return factor_of


def bell_draw(own_key, extent, deviation, limit, split=(), held_as=jnp.bfloat16):
    loudness = level_of(own_key, extent, split, -0.22, 0.18) if split else 1.0
    values = jax.random.normal(own_key, extent, jnp.float32) * deviation * loudness
    return jnp.minimum(jnp.maximum(values, -limit), limit).astype(held_as)


def setup_inputs(seed: int = 0) -> dict:
    arg_keys = jax.random.split(jax.random.key(seed), 14)
    node_coef = bell_draw(arg_keys[0], (ATOMS, NCOEF, C), 1.0, 6.0, ((0, 128),))
    cotangent = bell_draw(arg_keys[1], (ATOMS, NCOEF, C), 1.0, 6.0, ((0, 128),))
    wigner = draw_wigner(jax.random.fold_in(arg_keys[13], 71), 0)
    envelope = jnp.clip(jnp.exp(math.log(1.0) - 1.609438 * jax.random.uniform(arg_keys[3], (BLOCKS, EB), jnp.float32) ** level_of(arg_keys[3], (BLOCKS, EB), ((0, 128),), -0.2, 0.2)), 0.2, 1.0)
    src_tile = draw_src_tile(jax.random.fold_in(arg_keys[13], 71), 0)
    dst_tile = draw_dst_tile(jax.random.fold_in(arg_keys[13], 71), 0)
    src_slot = with_ends(jax.random.randint(arg_keys[6], (BLOCKS, EB), 0, TILE), jax.random.fold_in(arg_keys[6], 1), 0, TILE - 1).astype(jnp.int32)
    dst_slot = with_ends(jax.random.randint(arg_keys[7], (BLOCKS, EB), 0, TILE), jax.random.fold_in(arg_keys[7], 1), 0, TILE - 1).astype(jnp.int32)
    bucket = with_ends(jax.random.randint(arg_keys[8], (BLOCKS, EB), 0, BUCKETS), jax.random.fold_in(arg_keys[8], 1), 0, BUCKETS - 1).astype(jnp.int32)
    mask = draw_mask(jax.random.fold_in(arg_keys[13], 71), 0)
    w_zero = bell_draw(arg_keys[10], (7 * C, 7 * C), (7 * C) ** -0.5, 0.1875)
    w_one = bell_draw(arg_keys[11], (2, 6 * C, 6 * C), (12 * C) ** -0.5, 0.15625)
    w_two = bell_draw(arg_keys[12], (2, 5 * C, 5 * C), (10 * C) ** -0.5, 0.15625)
    return dict(node_coef=node_coef, cotangent=cotangent, wigner=wigner, envelope=envelope, src_tile=src_tile, dst_tile=dst_tile, src_slot=src_slot, dst_slot=dst_slot, bucket=bucket, mask=mask, w_zero=w_zero, w_one=w_one, w_two=w_two)


def complex_block(weights):
    upper_half = jnp.concatenate([weights[0], weights[1]], axis=1)
    lower_half = jnp.concatenate([-weights[1], weights[0]], axis=1)
    return jnp.concatenate([upper_half, lower_half], axis=0)

def turn(rotation, coef):
    return jnp.einsum('eij,ejc->eic', rotation.astype(jnp.float32), coef.astype(jnp.float32))

def turn_back(rotation, coef):
    return jnp.einsum('eji,ejc->eic', rotation.astype(jnp.float32), coef.astype(jnp.float32))

def so_two(rotated, w_zero, w_one, w_two):
    edge_count = rotated.shape[0]
    channels = rotated.shape[2]
    zero_part = rotated[:, :7].reshape(edge_count, 7 * channels)
    one_part = rotated[:, 7:19].reshape(edge_count, 12 * channels)
    two_part = rotated[:, 19:].reshape(edge_count, 10 * channels)
    out_zero = jnp.dot(zero_part, w_zero, preferred_element_type=jnp.float32)
    out_one = jnp.dot(one_part, complex_block(w_one), preferred_element_type=jnp.float32)
    out_two = jnp.dot(two_part, complex_block(w_two), preferred_element_type=jnp.float32)
    hidden = jnp.concatenate([out_zero.reshape(edge_count, 7, channels), out_one.reshape(edge_count, 12, channels), out_two.reshape(edge_count, 10, channels)], axis=1)
    return (hidden, (zero_part, one_part, two_part))

def so_two_back(grad_hidden, w_zero, w_one, w_two):
    edge_count = grad_hidden.shape[0]
    channels = grad_hidden.shape[2]
    grad_zero = grad_hidden[:, :7].reshape(edge_count, 7 * channels)
    grad_one = grad_hidden[:, 7:19].reshape(edge_count, 12 * channels)
    grad_two = grad_hidden[:, 19:].reshape(edge_count, 10 * channels)
    back_zero = jnp.dot(grad_zero, w_zero.T, preferred_element_type=jnp.float32)
    back_one = jnp.dot(grad_one, complex_block(w_one).T, preferred_element_type=jnp.float32)
    back_two = jnp.dot(grad_two, complex_block(w_two).T, preferred_element_type=jnp.float32)
    return jnp.concatenate([back_zero.reshape(edge_count, 7, channels), back_one.reshape(edge_count, 12, channels), back_two.reshape(edge_count, 10, channels)], axis=1)

def complex_grad(part, grad_part):
    half = part.shape[1] // 2
    outer = jnp.dot(part.T, grad_part, preferred_element_type=jnp.float32)
    real_grad = outer[:half, :half] + outer[half:, half:]
    imag_grad = outer[:half, half:] - outer[half:, :half]
    return jnp.stack([real_grad, imag_grad])

def weight_grads(parts, grad_hidden):
    edge_count = grad_hidden.shape[0]
    channels = grad_hidden.shape[2]
    grad_zero = grad_hidden[:, :7].reshape(edge_count, 7 * channels)
    grad_one = grad_hidden[:, 7:19].reshape(edge_count, 12 * channels)
    grad_two = grad_hidden[:, 19:].reshape(edge_count, 10 * channels)
    first_grad = jnp.dot(parts[0].T, grad_zero, preferred_element_type=jnp.float32)
    return (first_grad, complex_grad(parts[1], grad_one), complex_grad(parts[2], grad_two))

def gate_forward(hidden):
    scalar = hidden[:, 0]
    sigmoid_gate = jax.nn.sigmoid(scalar)
    return jnp.concatenate([(scalar * sigmoid_gate)[:, None], hidden[:, 1:] * sigmoid_gate[:, None]], axis=1)

def gate_backward(hidden, grad_gated):
    scalar = hidden[:, 0]
    sigmoid_gate = jax.nn.sigmoid(scalar)
    slope = sigmoid_gate * (1.0 - sigmoid_gate)
    grad_scalar = grad_gated[:, 0] * sigmoid_gate * (1.0 + scalar * (1.0 - sigmoid_gate))
    grad_scalar = grad_scalar + slope * lax.optimization_barrier(jnp.sum(grad_gated[:, 1:] * hidden[:, 1:], axis=1))
    return jnp.concatenate([grad_scalar[:, None], grad_gated[:, 1:] * sigmoid_gate[:, None]], axis=1)

def edge_forward(source_coef, rotation, edge_scale, w_zero, w_one, w_two):
    rotated = turn(rotation, source_coef).astype(jnp.bfloat16)
    hidden, parts = so_two(rotated, w_zero, w_one, w_two)
    gated = gate_forward(hidden).astype(jnp.bfloat16)
    message = (edge_scale[:, None, None] * turn_back(rotation, gated)).astype(jnp.bfloat16)
    return (message, (hidden, parts))

def edge_backward(saved, rotation, edge_scale, target_cot, w_zero, w_one, w_two):
    hidden, parts = saved
    grad_gated = edge_scale[:, None, None] * turn(rotation, target_cot)
    grad_hidden = gate_backward(hidden, grad_gated).astype(jnp.bfloat16)
    grad_rotated = so_two_back(grad_hidden, w_zero, w_one, w_two).astype(jnp.bfloat16)
    source_grad = turn_back(rotation, grad_rotated)
    return (source_grad, weight_grads(parts, grad_hidden))

def reference(node_coef, cotangent, wigner, envelope, src_tile, dst_tile, src_slot, dst_slot, bucket, mask, w_zero, w_one, w_two):
    channels = node_coef.shape[2]
    src_atom = (src_tile[:, None] * TILE + src_slot).astype(jnp.int32).reshape(N_GRAPH, -1)
    dst_atom = (dst_tile[:, None] * TILE + dst_slot).astype(jnp.int32).reshape(N_GRAPH, -1)
    edge_scale = (0.3 * envelope * mask.astype(jnp.float32)).reshape(N_GRAPH, -1)
    angle_kinds = bucket.astype(jnp.int32).reshape(N_GRAPH, -1)

    def owner_step(carry, inputs):
        agg_total, grad_total, zero_total, one_total, two_total = carry
        src_rows, dst_rows, scales, kinds = inputs
        rotation = wigner[kinds]
        message, saved = edge_forward(node_coef[src_rows], rotation, scales, w_zero, w_one, w_two)
        source_grad, grads = edge_backward(saved, rotation, scales, cotangent[dst_rows], w_zero, w_one, w_two)
        agg_total = agg_total.at[dst_rows].add(message.astype(jnp.float32))
        grad_total = grad_total.at[src_rows].add(source_grad)
        return ((agg_total, grad_total, zero_total + grads[0], one_total + grads[1], two_total + grads[2]), None)
    start = (jnp.zeros(node_coef.shape, jnp.float32), jnp.zeros(node_coef.shape, jnp.float32), jnp.zeros((7 * channels, 7 * channels), jnp.float32), jnp.zeros((2, 6 * channels, 6 * channels), jnp.float32), jnp.zeros((2, 5 * channels, 5 * channels), jnp.float32))
    final, unused = lax.scan(owner_step, start, (src_atom, dst_atom, edge_scale, angle_kinds))
    agg_total, grad_total, zero_total, one_total, two_total = final
    updated = (node_coef.astype(jnp.float32) + agg_total).astype(jnp.bfloat16)
    grad_coef = (cotangent.astype(jnp.float32) + grad_total).astype(jnp.bfloat16)
    return (updated, grad_coef, zero_total.reshape(-1), one_total.reshape(-1), two_total.reshape(-1))
```

```python
import jax
import jax.numpy as jnp
import numpy as np
from jax import lax
from jax.experimental import pallas as pl
from jax.experimental.pallas import tpu as pltpu
from jax.sharding import Mesh, PartitionSpec as P

BF = jnp.bfloat16
F32 = jnp.float32
NC = 29
C = 128
E = 768
CH = 256
STEPS = E // CH
TILE = 64
W = NC * C
PART_A = (0, 1, 2, 3, 7, 8, 9, 13, 14, 15, 19, 20, 24, 25)
PART_B = (4, 5, 6, 10, 11, 12, 16, 17, 18, 21, 22, 23, 26, 27, 28)
ROWS_ONE, ROWS_TWO, ROWS_ZERO = 72, 50, 49
AT_TWO, AT_ZERO, CHUNK = 80, 136, 192
VMEM = 62 * 1024 * 1024
COL_PAIRS = tuple((k, min(2, NC - k)) for k in range(0, NC, 2))


def dot(a, b):
    return jnp.dot(a, b, preferred_element_type=F32)


def dot_nt(a, b):
    return lax.dot_general(a, b, (((1,), (1,)), ((), ())), preferred_element_type=F32)


def place_matrix():
    place = np.zeros((NC, 256), np.float32)
    for part in (PART_A, PART_B):
        for spot, coef in enumerate(part):
            place[coef, spot * 16 : spot * 16 + 16] = 1.0
    return jnp.asarray(place, BF)


def table_kernel(pick_ref, fwd_ref, back_ref, out_fwd, out_back):
    row = lax.broadcasted_iota(jnp.int32, (E, 256), 0)
    lane = lax.broadcasted_iota(jnp.int32, (E, 256), 1)
    keep = (row % 16) == (lane % 16)
    for table, out in ((fwd_ref, out_fwd), (back_ref, out_back)):
        out[0] = jnp.where(keep, dot(pick_ref[...], table[0]), 0.0).astype(BF)


def gather_part(ref, rows, part):
    pieces = [ref[coef, rows, :] for coef in part]
    short = 16 - len(part)
    if short:
        pieces.append(jnp.zeros((16 * short, 256), BF))
    return jnp.concatenate(pieces, axis=0)


def turn_part(table_ref, table_rows, ref, rows, part):
    lhs = jnp.concatenate([table_ref[coef, table_rows, :] for coef in part], axis=0)
    return dot(lhs, gather_part(ref, rows, part))


def edge_kernel(
    core_ref,
    table_ref,
    src_ref,
    dst_ref,
    scale_ref,
    low_ref,
    own_ref,
    high_ref,
    w_zero_hbm,
    w_one_hbm,
    w_two_hbm,
    gated_hbm,
    grad_hbm,
    send_hbm,
    both,
    turned,
    rot,
    rot_t,
    grad,
    gated,
    scalar,
    first,
    total,
    w_zero,
    w_one,
    w_two,
    flat_a,
    flat_b,
    stage_one,
    stage_rest,
    sems,
):
    step = pl.program_id(0)

    def weight_copy(k):
        source, held = ((w_zero_hbm, w_zero), (w_one_hbm, w_one), (w_two_hbm, w_two))[k]
        return pltpu.make_async_copy(source, held, sems.at[k])

    @pl.when(step == 0)
    def _():
        for k in range(3):
            weight_copy(k).start()
        weight_copy(0).wait()

    for half, picker in ((0, src_ref), (1, dst_ref)):
        for start, width in COL_PAIRS:
            window = [
                jnp.concatenate(
                    [ref[half * NC + k] for ref in (low_ref, own_ref, high_ref)], axis=0
                )
                for k in range(start, start + width)
            ]
            picked = dot(picker[...], jnp.concatenate(window, axis=1)).astype(BF)
            for k in range(width):
                both[start + k, :, half * C : half * C + C] = picked[:, k * C : (k + 1) * C]

    base = pl.multiple_of(step * CH, CH)

    def turn_group(g, carry):
        rows = pl.ds(pl.multiple_of(g * 16, 16), 16)
        out_rows = pl.ds(pl.multiple_of(base + g * 16, 16), 16)
        for part in (PART_A, PART_B):
            out = turn_part(table_ref, rows, both, rows, part)
            for spot, coef in enumerate(part):
                piece = out[spot * 16 : spot * 16 + 16]
                rot[out_rows, coef * C : (coef + 1) * C] = piece[:, :C].astype(BF)
                turned[coef, rows, :] = piece[:, C:]
        return carry

    lax.fori_loop(0, CH // 16, turn_group, 0)

    here = pl.ds(base, CH)
    t = dot(rot[here, : 7 * C], w_zero[:, :C])
    scalar[here, :] = t
    edge_scale = scale_ref[...]
    first[here, :] = turned[0] * edge_scale
    factor = jax.nn.sigmoid(t) * edge_scale
    for coef in range(1, NC):
        grad[here, coef * C : (coef + 1) * C] = (turned[coef] * factor).astype(BF)
    for coef in range(NC):
        rot_t[coef * C : (coef + 1) * C, here] = rot[here, coef * C : (coef + 1) * C].T

    @pl.when(step == STEPS - 1)
    def _():
        weight_copy(1).wait()
        weight_copy(2).wait()
        total[...] = jnp.zeros_like(total)

        def gate(hidden, coef, count):
            sig = jax.nn.sigmoid(scalar[...])
            for k in range(count):
                value = hidden[:, k * C : (k + 1) * C]
                gated[coef + k] = (value * sig).astype(BF)
                if not (isinstance(coef, int) and coef + k == 0):
                    lanes = pl.ds(pl.multiple_of((coef + k) * C, C), C)
                    total[...] += value * grad[:, lanes].astype(F32)

        for n in range(4):
            width = 2 if n < 3 else 1
            gate(
                dot(rot[:, : 7 * C], w_zero[:, 2 * n * C : (2 * n + width) * C]), 2 * n, width
            )

        def so_two(weights, begin, half):
            mid = begin + half

            def run(lanes, n, width):
                plus = rot[:, begin * C : mid * C]
                minus = rot[:, mid * C : (mid + half) * C]
                gate(dot(plus, weights[0, :, lanes]) - dot(minus, weights[1, :, lanes]), begin + 2 * n, width)
                gate(dot(minus, weights[0, :, lanes]) + dot(plus, weights[1, :, lanes]), mid + 2 * n, width)

            def body(n, carry):
                run(pl.ds(pl.multiple_of(n * 256, 256), 256), n, 2)
                return carry

            lax.fori_loop(0, half // 2, body, 0)
            if half % 2:
                run(slice((half - 1) * C, half * C), half // 2, 1)

        so_two(w_one, 7, 6)
        so_two(w_two, 19, 5)

        t_all = scalar[...]
        sig = jax.nn.sigmoid(t_all)
        rest = 1.0 - sig
        grad[:, :C] = (first[...] * sig * (1.0 + t_all * rest) + rest * total[...]).astype(BF)

        out_gated = pltpu.make_async_copy(gated, gated_hbm, sems.at[3])
        out_grad = pltpu.make_async_copy(grad, grad_hbm, sems.at[4])
        out_gated.start()
        out_grad.start()

        core = core_ref[0]

        def spread(value, flat, tile, width, tiles):
            rows = value.shape[0]
            for k in range(width):
                flat[pl.ds(tile + k, rows, stride=tiles), :] = value[:, k * C : (k + 1) * C]

        def pairs(begin, half):
            plus, minus = slice(begin * C, (begin + half) * C), slice((begin + half) * C, (begin + 2 * half) * C)
            return rot_t[plus, :], rot_t[minus, :], begin * C, (begin + half) * C

        def pack_one(first_chip):
            def body(chip, carry):
                for parity in range(2):
                    at = pl.multiple_of((2 * chip + parity) * ROWS_ONE, 8)
                    stage_one[jnp.bitwise_xor(core, parity), first_chip + chip] = flat_a[
                        pl.ds(at, AT_TWO), :
                    ].astype(BF)
                return carry

            lax.fori_loop(0, 32, body, 0)

        plus, minus, at_p, at_m = pairs(7, 6)
        for n in range(3):
            g_p = grad[:, at_p + n * 256 : at_p + (n + 1) * 256]
            g_m = grad[:, at_m + n * 256 : at_m + (n + 1) * 256]
            spread(dot(plus, g_p) + dot(minus, g_m), flat_a, 2 * n, 2, 6)
        pack_one(0)
        for n in range(3):
            g_p = grad[:, at_p + n * 256 : at_p + (n + 1) * 256]
            g_m = grad[:, at_m + n * 256 : at_m + (n + 1) * 256]
            spread(dot(plus, g_m) - dot(minus, g_p), flat_a, 2 * n, 2, 6)
        pack_one(32)
        out_one = pltpu.make_async_copy(stage_one, send_hbm.at[:, :, :AT_TWO], sems.at[5])
        out_one.start()

        plus = rot_t[: 7 * C, :]
        for n in range(4):
            width = 2 if n < 3 else 1
            spread(dot(plus, grad[:, n * 256 : n * 256 + width * C]), flat_a, 2 * n, width, 7)

        def pack_rest(first_chip):
            def body(chip, carry):
                for parity in range(2):
                    device = 2 * chip + parity
                    two = flat_b[pl.ds(device * ROWS_TWO, 56), :]
                    zero = flat_a[pl.ds((2 * first_chip + device) * ROWS_ZERO, 56), :]
                    stage_rest[jnp.bitwise_xor(core, parity), first_chip + chip] = (
                        jnp.concatenate([two, zero], axis=0).astype(BF)
                    )
                return carry

            lax.fori_loop(0, 32, body, 0)

        plus, minus, at_p, at_m = pairs(19, 5)
        for imaginary in (False, True):
            for n in range(3):
                width = 2 if n < 2 else 1
                g_p = grad[:, at_p + n * 256 : at_p + n * 256 + width * C]
                g_m = grad[:, at_m + n * 256 : at_m + n * 256 + width * C]
                if imaginary:
                    value = dot(plus, g_m) - dot(minus, g_p)
                else:
                    value = dot(plus, g_p) + dot(minus, g_m)
                spread(value, flat_b, 2 * n, width, 5)
            pack_rest(32 if imaginary else 0)
        out_rest = pltpu.make_async_copy(stage_rest, send_hbm.at[:, :, AT_TWO:], sems.at[6])
        out_rest.start()
        for copy in (out_gated, out_grad, out_one, out_rest):
            copy.wait()


def back_kernel(
    table_ref,
    scale_ref,
    src_ref,
    dst_ref,
    w_zero_hbm,
    w_one_hbm,
    w_two_hbm,
    gated_hbm,
    grad_hbm,
    low_ref,
    own_ref,
    high_ref,
    both,
    grad,
    message,
    source,
    w_zero,
    w_one,
    w_two,
    sems,
):
    step = pl.program_id(0)

    @pl.when(step == 0)
    def _():
        copies = [
            pltpu.make_async_copy(grad_hbm, grad, sems.at[0]),
            pltpu.make_async_copy(w_zero_hbm, w_zero, sems.at[1]),
            pltpu.make_async_copy(w_one_hbm, w_one, sems.at[2]),
            pltpu.make_async_copy(w_two_hbm, w_two, sems.at[3]),
            pltpu.make_async_copy(gated_hbm, both.at[:, :, :C], sems.at[4]),
        ]
        for copy in copies:
            copy.start()
        copies[0].wait()
        copies[1].wait()

        def put(value, coef, count):
            for k in range(count):
                both[coef + k, :, C:] = value[:, k * C : (k + 1) * C].astype(BF)

        for n in range(4):
            width = 2 if n < 3 else 1
            put(dot_nt(grad[:, : 7 * C], w_zero[2 * n * C : (2 * n + width) * C, :]), 2 * n, width)

        def so_two_back(weights, begin, half):
            mid = begin + half

            def run(rows, n, width):
                plus = grad[:, begin * C : mid * C]
                minus = grad[:, mid * C : (mid + half) * C]
                put(dot_nt(plus, weights[0, rows, :]) + dot_nt(minus, weights[1, rows, :]), begin + 2 * n, width)
                put(dot_nt(minus, weights[0, rows, :]) - dot_nt(plus, weights[1, rows, :]), mid + 2 * n, width)

            def body(n, carry):
                run(pl.ds(pl.multiple_of(n * 256, 256), 256), n, 2)
                return carry

            lax.fori_loop(0, half // 2, body, 0)
            if half % 2:
                run(slice((half - 1) * C, half * C), half // 2, 1)

        copies[2].wait()
        so_two_back(w_one, 7, 6)
        copies[3].wait()
        so_two_back(w_two, 19, 5)
        copies[4].wait()

    base = pl.multiple_of(step * CH, CH)

    def turn_group(g, carry):
        rows = pl.ds(pl.multiple_of(g * 16, 16), 16)
        out_rows = pl.ds(pl.multiple_of(base + g * 16, 16), 16)
        edge_scale = scale_ref[rows, :]
        for part in (PART_A, PART_B):
            out = turn_part(table_ref, rows, both, out_rows, part)
            for spot, coef in enumerate(part):
                piece = out[spot * 16 : spot * 16 + 16]
                lanes = slice(coef * C, (coef + 1) * C)
                message[out_rows, lanes] = (piece[:, :C] * edge_scale).astype(BF)
                source[out_rows, lanes] = piece[:, C:].astype(BF)
        return carry

    lax.fori_loop(0, CH // 16, turn_group, 0)

    @pl.when(step == STEPS - 1)
    def _():
        for half, picker, values in ((0, dst_ref, message), (1, src_ref, source)):
            for start, width in COL_PAIRS:
                summed = dot(picker[...], values[:, start * C : (start + width) * C])
                for k in range(width):
                    at = half * NC + start + k
                    piece = summed[:, k * C : (k + 1) * C]
                    low_ref[at] = piece[:TILE].astype(BF)
                    own_ref[at] = piece[TILE : 2 * TILE]
                    high_ref[at] = piece[2 * TILE :].astype(BF)


def whole(shape):
    return pl.BlockSpec(shape, lambda *_: (0,) * len(shape), pipeline_mode=pl.Buffered(1))


def shift(value, steps):
    count = lax.axis_size("chip") * 2
    pairs = [(i, i + steps) for i in range(count) if 0 <= i + steps < count]
    return lax.ppermute(value, ("chip", "core"), pairs)


def local(
    node_coef,
    cotangent,
    wigner,
    envelope,
    src_tile,
    dst_tile,
    src_slot,
    dst_slot,
    bucket,
    mask,
    w_zero,
    w_one,
    w_two,
):
    core = lax.axis_index("core")
    device = lax.axis_index("chip") * 2 + core
    own = jnp.concatenate(
        [node_coef.transpose(1, 0, 2), cotangent.transpose(1, 0, 2)], axis=0
    )
    low = shift(own, 1)
    high = shift(own, -1)

    src_index = ((src_tile - (device - 1))[:, None] * TILE + src_slot).reshape(-1)
    dst_index = ((dst_tile - (device - 1))[:, None] * TILE + dst_slot).reshape(-1)
    edge_scale = (0.3 * envelope * mask.astype(F32)).reshape(-1)
    scale = jnp.broadcast_to(edge_scale[:, None], (E, C))
    window = jnp.arange(3 * TILE, dtype=jnp.int32)
    src_pick = (src_index[:, None] == window[None, :]).astype(BF)
    dst_pick = (dst_index[:, None] == window[None, :]).astype(BF)
    src_put = (window[:, None] == src_index[None, :]).astype(BF)
    dst_put = (window[:, None] == dst_index[None, :]).astype(BF)
    kinds = wigner.shape[0]
    kind_pick = (bucket.reshape(-1)[:, None] == jnp.arange(kinds, dtype=jnp.int32)).astype(BF)

    place = place_matrix()
    by_kind = wigner.transpose(1, 2, 0)
    fwd_rows = jnp.einsum("ijb,jl->ibl", by_kind, place, preferred_element_type=F32).astype(BF)
    back_rows = jnp.einsum("ijb,il->jbl", by_kind, place, preferred_element_type=F32).astype(BF)
    table_shape = jax.ShapeDtypeStruct((NC, E, 256), BF)
    fwd_table, back_table = pl.pallas_call(
        table_kernel,
        grid=(NC,),
        in_specs=[
            whole((E, kinds)),
            pl.BlockSpec((1, kinds, 256), lambda i: (i, 0, 0)),
            pl.BlockSpec((1, kinds, 256), lambda i: (i, 0, 0)),
        ],
        out_specs=[pl.BlockSpec((1, E, 256), lambda i: (i, 0, 0))] * 2,
        out_shape=[table_shape] * 2,
        cost_estimate=pl.CostEstimate(
            flops=4 * NC * E * 256 * 256, bytes_accessed=4 * NC * E * 256, transcendentals=0
        ),
        name="rotation_tables",
    )(kind_pick, fwd_rows, back_rows)

    anywhere = pl.BlockSpec(memory_space=pl.ANY)
    halo = whole((2 * NC, TILE, C))
    table_block = pl.BlockSpec((NC, CH, 256), lambda s: (0, s, 0))
    scale_block = pl.BlockSpec((CH, C), lambda s: (s, 0))
    weight_scratch = [
        pltpu.VMEM(w_zero.shape, BF),
        pltpu.VMEM(w_one.shape, BF),
        pltpu.VMEM(w_two.shape, BF),
    ]
    gated, grad, send = pl.pallas_call(
        edge_kernel,
        grid=(STEPS,),
        in_specs=[
            pl.BlockSpec(memory_space=pltpu.SMEM),
            table_block,
            pl.BlockSpec((CH, 3 * TILE), lambda s: (s, 0)),
            pl.BlockSpec((CH, 3 * TILE), lambda s: (s, 0)),
            scale_block,
            halo,
            halo,
            halo,
            anywhere,
            anywhere,
            anywhere,
        ],
        out_specs=[anywhere] * 3,
        out_shape=[
            jax.ShapeDtypeStruct((NC, E, C), BF),
            jax.ShapeDtypeStruct((E, W), BF),
            jax.ShapeDtypeStruct((2, 64, CHUNK, C), BF),
        ],
        scratch_shapes=[
            pltpu.VMEM((NC, CH, 2 * C), BF),
            pltpu.VMEM((NC, CH, C), F32),
            pltpu.VMEM((E, W), BF),
            pltpu.VMEM((W, E), BF),
            pltpu.VMEM((E, W), BF),
            pltpu.VMEM((NC, E, C), BF),
            pltpu.VMEM((E, C), F32),
            pltpu.VMEM((E, C), F32),
            pltpu.VMEM((E, C), F32),
            *weight_scratch,
            pltpu.VMEM((6280, C), F32),
            pltpu.VMEM((3208, C), F32),
            pltpu.VMEM((2, 64, AT_TWO, C), BF),
            pltpu.VMEM((2, 64, CHUNK - AT_TWO, C), BF),
            pltpu.SemaphoreType.DMA((7,)),
        ],
        compiler_params=pltpu.CompilerParams(vmem_limit_bytes=VMEM),
        cost_estimate=pl.CostEstimate(
            flops=20_000_000_000, bytes_accessed=40_000_000, transcendentals=0
        ),
        name="edges_and_weight_grads",
    )(
        core.astype(jnp.int32).reshape(1),
        fwd_table,
        src_pick,
        dst_pick,
        scale,
        low,
        own,
        high,
        w_zero,
        w_one,
        w_two,
    )

    other = lax.ppermute(send[1], "core", [(0, 1), (1, 0)])
    paired = (send[0].astype(F32) + other.astype(F32)).astype(BF)
    exchanged = lax.all_to_all(paired, "chip", 0, 0)

    halo_shape = (2 * NC, TILE, C)
    to_low, centre, to_high = pl.pallas_call(
        back_kernel,
        grid=(STEPS,),
        in_specs=[
            table_block,
            scale_block,
            whole((3 * TILE, E)),
            whole((3 * TILE, E)),
            anywhere,
            anywhere,
            anywhere,
            anywhere,
            anywhere,
        ],
        out_specs=[pl.BlockSpec(halo_shape, lambda s: (0, 0, 0))] * 3,
        out_shape=[
            jax.ShapeDtypeStruct(halo_shape, BF),
            jax.ShapeDtypeStruct(halo_shape, F32),
            jax.ShapeDtypeStruct(halo_shape, BF),
        ],
        scratch_shapes=[
            pltpu.VMEM((NC, E, 2 * C), BF),
            pltpu.VMEM((E, W), BF),
            pltpu.VMEM((E, W), BF),
            pltpu.VMEM((E, W), BF),
            *weight_scratch,
            pltpu.SemaphoreType.DMA((5,)),
        ],
        compiler_params=pltpu.CompilerParams(vmem_limit_bytes=VMEM),
        cost_estimate=pl.CostEstimate(
            flops=20_000_000_000, bytes_accessed=40_000_000, transcendentals=0
        ),
        name="edges_back",
    )(back_table, scale, src_put, dst_put, w_zero, w_one, w_two, gated, grad)

    from_high = shift(to_low, -1)
    from_low = shift(to_high, 1)
    result = (
        own.astype(F32) + (centre + from_high.astype(F32) + from_low.astype(F32))
    ).astype(BF)
    updated = result[:NC].transpose(1, 0, 2)
    grad_coef = result[NC:].transpose(1, 0, 2)

    sums = jnp.sum(exchanged.astype(F32), axis=0)
    grad_one = sums[:ROWS_ONE].reshape(-1)
    grad_two = sums[AT_TWO : AT_TWO + ROWS_TWO].reshape(-1)
    grad_zero = sums[AT_ZERO : AT_ZERO + ROWS_ZERO].reshape(-1)
    return (updated, grad_coef, grad_zero, grad_one, grad_two)


def solution(mesh):
    fine = Mesh(mesh.devices.reshape(-1, 2), ("chip", "core"))
    both = ("chip", "core")
    rows3, rows2 = P(both, None, None), P(both, None)
    in_specs = (rows3, rows3, P(), rows2, P(both), P(both), rows2, rows2, rows2, rows2, P(), P(), P())
    out_specs = (rows3, rows3, P(both), P(both), P(both))
    return jax.shard_map(local, mesh=fine, in_specs=in_specs, out_specs=out_specs, check_vma=False)
```

```python
import jax
import jax.numpy as jnp
import numpy as np
from jax import lax
from jax.experimental import pallas as pl
from jax.experimental.pallas import tpu as pltpu
from jax.sharding import Mesh, PartitionSpec as P

BF = jnp.bfloat16
F32 = jnp.float32
NC = 29
C = 128
E = 768
CH = 256
STEPS = E // CH
TILE = 64
W = NC * C
PARTS = (
    (1, 7, 13, 2, 8, 14, 19, 24),
    (0, 3, 9, 15, 20, 25),
    (4, 10, 16, 21, 26),
    (5, 11, 17, 22, 27),
    (6, 12, 18, 23, 28),
)
ROWS_ONE, ROWS_TWO, ROWS_ZERO = 72, 50, 49
AT_TWO, AT_ZERO, CHUNK = 80, 136, 192
TABLE_STEP = 4
VMEM = 62 * 1024 * 1024
COL_PAIRS = tuple((k, min(2, NC - k)) for k in range(0, NC, 2))


def dot(a, b):
    return jnp.dot(a, b, preferred_element_type=F32)


def dot_nt(a, b):
    return lax.dot_general(a, b, (((1,), (1,)), ((), ())), preferred_element_type=F32)


def place_matrix():
    place = np.zeros((NC, C), np.float32)
    for part in PARTS:
        for spot, coef in enumerate(part):
            place[coef, spot * 16 : spot * 16 + 16] = 1.0
    return jnp.asarray(place, BF)


def prepare_kernel(
    first_ref,
    src_tile,
    dst_tile,
    src_slot,
    dst_slot,
    bucket,
    envelope,
    mask,
    src_pick,
    dst_pick,
    src_put,
    dst_put,
    kind_pick,
    scale,
):
    first = first_ref[0]
    window = lax.broadcasted_iota(jnp.int32, (3 * TILE, C), 0)
    kind = lax.broadcasted_iota(jnp.int32, (kind_pick.shape[1], C), 0)
    for k in range(E // C):
        blocks = (2 * k, 2 * k + 1)
        edges = slice(k * C, (k + 1) * C)

        def row(ref):
            return jnp.concatenate([ref[b : b + 1, :] for b in blocks], axis=1)

        for tile, slot, pick, put in (
            (src_tile, src_slot, src_pick, src_put),
            (dst_tile, dst_slot, dst_pick, dst_put),
        ):
            index = jnp.concatenate(
                [slot[b : b + 1, :] + (tile[b] - first) * TILE for b in blocks], axis=1
            )
            hit = jnp.where(window == index, 1.0, 0.0)
            put[:, edges] = hit.astype(BF)
            pick[edges, :] = hit.T.astype(BF)
        kind_pick[edges, :] = jnp.where(kind == row(bucket), 1.0, 0.0).T.astype(BF)
        weight = 0.3 * row(envelope) * row(mask).astype(F32)
        scale[edges, :] = jnp.broadcast_to(weight, (C, C)).T


def table_kernel(pick_ref, rows_ref, out):
    row = lax.broadcasted_iota(jnp.int32, (E, 2 * C), 0)
    lane = lax.broadcasted_iota(jnp.int32, (E, 2 * C), 1)
    keep = jnp.where((row % 16) == (lane % 16), 1.0, 0.0).astype(BF)
    for k in range(0, TABLE_STEP, 2):
        pair = jnp.concatenate([rows_ref[k], rows_ref[k + 1]], axis=1)
        value = dot(pick_ref[...], pair).astype(BF) * keep
        out[k] = value[:, :C]
        out[k + 1] = value[:, C:]


def rotation_table(kind_pick, rows, name):
    kinds = kind_pick.shape[1]
    return pl.pallas_call(
        table_kernel,
        grid=(pl.cdiv(NC, TABLE_STEP),),
        in_specs=[
            whole((E, kinds)),
            pl.BlockSpec((TABLE_STEP, kinds, C), lambda i: (i, 0, 0)),
        ],
        out_specs=pl.BlockSpec((TABLE_STEP, E, C), lambda i: (i, 0, 0)),
        out_shape=jax.ShapeDtypeStruct((NC, E, C), BF),
        cost_estimate=pl.CostEstimate(
            flops=NC * E * C * 1024, bytes_accessed=4 * NC * E * C, transcendentals=0
        ),
        name=name,
    )(kind_pick, rows)


def gather_part(ref, rows, part):
    pieces = [ref[coef, rows, :] for coef in part]
    short = 8 - len(part)
    if short:
        pieces.append(jnp.zeros((16 * short, 256), BF))
    return jnp.concatenate(pieces, axis=0)


def turn_part(table_ref, table_rows, ref, rows, part):
    lhs = jnp.concatenate([table_ref[coef, table_rows, :] for coef in part], axis=0)
    return dot(lhs, gather_part(ref, rows, part))


def edge_kernel(
    core_ref,
    table_ref,
    src_ref,
    dst_ref,
    scale_ref,
    low_ref,
    own_ref,
    high_ref,
    w_zero_hbm,
    w_one_hbm,
    w_two_hbm,
    gated_hbm,
    grad_hbm,
    keep_hbm,
    send_hbm,
    both,
    turned,
    rot,
    rot_t,
    grad,
    gated,
    scalar,
    first,
    total,
    w_zero,
    w_one,
    w_two,
    flat_a,
    flat_b,
    stage_one,
    stage_rest,
    sems,
):
    step = pl.program_id(0)

    def weight_copy(k):
        source, held = ((w_zero_hbm, w_zero), (w_one_hbm, w_one), (w_two_hbm, w_two))[k]
        return pltpu.make_async_copy(source, held, sems.at[k])

    @pl.when(step == 0)
    def _():
        for k in range(3):
            weight_copy(k).start()
        weight_copy(0).wait()

    for half, picker in ((0, src_ref), (1, dst_ref)):
        for start, width in COL_PAIRS:
            window = [
                jnp.concatenate(
                    [ref[half * NC + k] for ref in (low_ref, own_ref, high_ref)], axis=0
                )
                for k in range(start, start + width)
            ]
            picked = dot(picker[...], jnp.concatenate(window, axis=1)).astype(BF)
            for k in range(width):
                both[start + k, :, half * C : half * C + C] = picked[:, k * C : (k + 1) * C]

    base = pl.multiple_of(step * CH, CH)

    def turn_group(g, carry):
        rows = pl.ds(pl.multiple_of(g * 16, 16), 16)
        out_rows = pl.ds(pl.multiple_of(base + g * 16, 16), 16)
        for part in PARTS:
            out = turn_part(table_ref, rows, both, rows, part)
            for spot, coef in enumerate(part):
                piece = out[spot * 16 : spot * 16 + 16]
                rot[out_rows, coef * C : (coef + 1) * C] = piece[:, :C].astype(BF)
                turned[coef, rows, :] = piece[:, C:]
        return carry

    lax.fori_loop(0, CH // 16, turn_group, 0, unroll=CH // 16)

    here = pl.ds(base, CH)
    t = dot(rot[here, : 7 * C], w_zero[:, :C])
    scalar[here, :] = t
    edge_scale = scale_ref[...]
    first[here, :] = turned[0] * edge_scale
    factor = jax.nn.sigmoid(t) * edge_scale
    for coef in range(1, NC):
        grad[here, coef * C : (coef + 1) * C] = (turned[coef] * factor).astype(BF)
    for coef in range(NC):
        rot_t[coef * C : (coef + 1) * C, here] = rot[here, coef * C : (coef + 1) * C].T

    @pl.when(step == STEPS - 1)
    def _():
        weight_copy(1).wait()
        weight_copy(2).wait()
        total[...] = jnp.zeros_like(total)

        def gate(hidden, coef, count):
            sig = jax.nn.sigmoid(scalar[...])
            for k in range(count):
                value = hidden[:, k * C : (k + 1) * C]
                gated[coef + k] = (value * sig).astype(BF)
                if not (isinstance(coef, int) and coef + k == 0):
                    lanes = pl.ds(pl.multiple_of((coef + k) * C, C), C)
                    total[...] += value * grad[:, lanes].astype(F32)

        for n in range(4):
            width = 2 if n < 3 else 1
            gate(
                dot(rot[:, : 7 * C], w_zero[:, 2 * n * C : (2 * n + width) * C]), 2 * n, width
            )

        def so_two(weights, begin, half):
            mid = begin + half

            def run(lanes, n, width):
                plus = rot[:, begin * C : mid * C]
                minus = rot[:, mid * C : (mid + half) * C]
                gate(dot(plus, weights[0, :, lanes]) - dot(minus, weights[1, :, lanes]), begin + 2 * n, width)
                gate(dot(minus, weights[0, :, lanes]) + dot(plus, weights[1, :, lanes]), mid + 2 * n, width)

            def body(n, carry):
                run(pl.ds(pl.multiple_of(n * 256, 256), 256), n, 2)
                return carry

            lax.fori_loop(0, half // 2, body, 0)
            if half % 2:
                run(slice((half - 1) * C, half * C), half // 2, 1)

        so_two(w_one, 7, 6)
        so_two(w_two, 19, 5)

        t_all = scalar[...]
        sig = jax.nn.sigmoid(t_all)
        rest = 1.0 - sig
        grad[:, :C] = (first[...] * sig * (1.0 + t_all * rest) + rest * total[...]).astype(BF)

        out_gated = pltpu.make_async_copy(gated, gated_hbm, sems.at[3])
        out_grad = pltpu.make_async_copy(grad, grad_hbm, sems.at[4])
        out_gated.start()
        out_grad.start()

        core = core_ref[0]

        def spread(value, flat, tile, width, tiles):
            rows = value.shape[0]
            for k in range(width):
                flat[pl.ds(tile + k, rows, stride=tiles), :] = value[:, k * C : (k + 1) * C]

        def pairs(begin, half):
            plus, minus = slice(begin * C, (begin + half) * C), slice((begin + half) * C, (begin + 2 * half) * C)
            return rot_t[plus, :], rot_t[minus, :], begin * C, (begin + half) * C

        def pack_one(first_chip):
            def body(chip, carry):
                for parity in range(2):
                    at = pl.multiple_of((2 * chip + parity) * ROWS_ONE, 8)
                    stage_one[jnp.bitwise_xor(core, parity), first_chip + chip] = flat_a[
                        pl.ds(at, AT_TWO), :
                    ].astype(BF)
                return carry

            lax.fori_loop(0, 32, body, 0, unroll=8)

        plus, minus, at_p, at_m = pairs(7, 6)
        for n in range(3):
            g_p = grad[:, at_p + n * 256 : at_p + (n + 1) * 256]
            g_m = grad[:, at_m + n * 256 : at_m + (n + 1) * 256]
            spread(dot(plus, g_p) + dot(minus, g_m), flat_a, 2 * n, 2, 6)
        pack_one(0)
        for n in range(3):
            g_p = grad[:, at_p + n * 256 : at_p + (n + 1) * 256]
            g_m = grad[:, at_m + n * 256 : at_m + (n + 1) * 256]
            spread(dot(plus, g_m) - dot(minus, g_p), flat_a, 2 * n, 2, 6)
        pack_one(32)
        outs = [
            pltpu.make_async_copy(stage_one.at[0], keep_hbm.at[:, :AT_TWO], sems.at[5]),
            pltpu.make_async_copy(stage_one.at[1], send_hbm.at[:, :AT_TWO], sems.at[6]),
            pltpu.make_async_copy(stage_rest.at[0], keep_hbm.at[:, AT_TWO:], sems.at[7]),
            pltpu.make_async_copy(stage_rest.at[1], send_hbm.at[:, AT_TWO:], sems.at[8]),
        ]
        outs[0].start()
        outs[1].start()

        plus = rot_t[: 7 * C, :]
        for n in range(4):
            width = 2 if n < 3 else 1
            spread(dot(plus, grad[:, n * 256 : n * 256 + width * C]), flat_a, 2 * n, width, 7)

        def pack_rest(first_chip):
            def body(chip, carry):
                for parity in range(2):
                    device = 2 * chip + parity
                    two = flat_b[pl.ds(device * ROWS_TWO, 56), :]
                    zero = flat_a[pl.ds((2 * first_chip + device) * ROWS_ZERO, 56), :]
                    stage_rest[jnp.bitwise_xor(core, parity), first_chip + chip] = (
                        jnp.concatenate([two, zero], axis=0).astype(BF)
                    )
                return carry

            lax.fori_loop(0, 32, body, 0, unroll=8)

        plus, minus, at_p, at_m = pairs(19, 5)
        for imaginary in (False, True):
            for n in range(3):
                width = 2 if n < 2 else 1
                g_p = grad[:, at_p + n * 256 : at_p + n * 256 + width * C]
                g_m = grad[:, at_m + n * 256 : at_m + n * 256 + width * C]
                if imaginary:
                    value = dot(plus, g_m) - dot(minus, g_p)
                else:
                    value = dot(plus, g_p) + dot(minus, g_m)
                spread(value, flat_b, 2 * n, width, 5)
            pack_rest(32 if imaginary else 0)
        outs[2].start()
        outs[3].start()
        for copy in (out_gated, out_grad, *outs):
            copy.wait()


def back_kernel(
    table_ref,
    scale_ref,
    src_ref,
    dst_ref,
    w_zero_hbm,
    w_one_hbm,
    w_two_hbm,
    gated_hbm,
    grad_hbm,
    low_ref,
    own_ref,
    high_ref,
    both,
    grad,
    message,
    source,
    w_zero,
    w_one,
    w_two,
    sems,
):
    step = pl.program_id(0)

    @pl.when(step == 0)
    def _():
        copies = [
            pltpu.make_async_copy(grad_hbm, grad, sems.at[0]),
            pltpu.make_async_copy(w_zero_hbm, w_zero, sems.at[1]),
            pltpu.make_async_copy(w_one_hbm, w_one, sems.at[2]),
            pltpu.make_async_copy(w_two_hbm, w_two, sems.at[3]),
            pltpu.make_async_copy(gated_hbm, both.at[:, :, :C], sems.at[4]),
        ]
        for copy in copies:
            copy.start()
        copies[0].wait()
        copies[1].wait()

        def put(value, coef, count):
            for k in range(count):
                both[coef + k, :, C:] = value[:, k * C : (k + 1) * C].astype(BF)

        for n in range(4):
            width = 2 if n < 3 else 1
            put(dot_nt(grad[:, : 7 * C], w_zero[2 * n * C : (2 * n + width) * C, :]), 2 * n, width)

        def so_two_back(weights, begin, half):
            mid = begin + half

            def run(rows, n, width):
                plus = grad[:, begin * C : mid * C]
                minus = grad[:, mid * C : (mid + half) * C]
                put(dot_nt(plus, weights[0, rows, :]) + dot_nt(minus, weights[1, rows, :]), begin + 2 * n, width)
                put(dot_nt(minus, weights[0, rows, :]) - dot_nt(plus, weights[1, rows, :]), mid + 2 * n, width)

            def body(n, carry):
                run(pl.ds(pl.multiple_of(n * 256, 256), 256), n, 2)
                return carry

            lax.fori_loop(0, half // 2, body, 0)
            if half % 2:
                run(slice((half - 1) * C, half * C), half // 2, 1)

        copies[2].wait()
        so_two_back(w_one, 7, 6)
        copies[3].wait()
        so_two_back(w_two, 19, 5)
        copies[4].wait()

    base = pl.multiple_of(step * CH, CH)

    def turn_group(g, carry):
        rows = pl.ds(pl.multiple_of(g * 16, 16), 16)
        out_rows = pl.ds(pl.multiple_of(base + g * 16, 16), 16)
        edge_scale = scale_ref[rows, :]
        for part in PARTS:
            out = turn_part(table_ref, rows, both, out_rows, part)
            for spot, coef in enumerate(part):
                piece = out[spot * 16 : spot * 16 + 16]
                lanes = slice(coef * C, (coef + 1) * C)
                message[out_rows, lanes] = (piece[:, :C] * edge_scale).astype(BF)
                source[out_rows, lanes] = piece[:, C:].astype(BF)
        return carry

    lax.fori_loop(0, CH // 16, turn_group, 0, unroll=CH // 16)

    @pl.when(step == STEPS - 1)
    def _():
        for half, picker, values in ((0, dst_ref, message), (1, src_ref, source)):
            for start, width in COL_PAIRS:
                summed = dot(picker[...], values[:, start * C : (start + width) * C])
                for k in range(width):
                    at = half * NC + start + k
                    piece = summed[:, k * C : (k + 1) * C]
                    low_ref[at] = piece[:TILE].astype(BF)
                    own_ref[at] = piece[TILE : 2 * TILE]
                    high_ref[at] = piece[2 * TILE :].astype(BF)


def whole(shape):
    return pl.BlockSpec(shape, lambda *_: (0,) * len(shape), pipeline_mode=pl.Buffered(1))


def shift(value, steps):
    count = lax.axis_size("chip") * 2
    pairs = [(i, i + steps) for i in range(count) if 0 <= i + steps < count]
    return lax.ppermute(value, ("chip", "core"), pairs)


def local(
    node_coef,
    cotangent,
    wigner,
    envelope,
    src_tile,
    dst_tile,
    src_slot,
    dst_slot,
    bucket,
    mask,
    w_zero,
    w_one,
    w_two,
):
    core = lax.axis_index("core")
    device = lax.axis_index("chip") * 2 + core
    own = jnp.concatenate(
        [node_coef.transpose(1, 0, 2), cotangent.transpose(1, 0, 2)], axis=0
    )
    low = shift(own, 1)
    high = shift(own, -1)

    kinds = wigner.shape[0]
    smem = pl.BlockSpec(memory_space=pltpu.SMEM)
    vmem = pl.BlockSpec(memory_space=pltpu.VMEM)
    src_pick, dst_pick, src_put, dst_put, kind_pick, scale = pl.pallas_call(
        prepare_kernel,
        in_specs=[smem, smem, smem, vmem, vmem, vmem, vmem, vmem],
        out_specs=[vmem] * 6,
        out_shape=[
            jax.ShapeDtypeStruct((E, 3 * TILE), BF),
            jax.ShapeDtypeStruct((E, 3 * TILE), BF),
            jax.ShapeDtypeStruct((3 * TILE, E), BF),
            jax.ShapeDtypeStruct((3 * TILE, E), BF),
            jax.ShapeDtypeStruct((E, kinds), BF),
            jax.ShapeDtypeStruct((E, C), F32),
        ],
        name="prepare",
    )(
        (device - 1).astype(jnp.int32).reshape(1),
        src_tile,
        dst_tile,
        src_slot,
        dst_slot,
        bucket,
        envelope,
        mask,
    )

    place = place_matrix()
    by_kind = wigner.transpose(1, 2, 0)
    fwd_rows = jnp.einsum("ijb,jl->ibl", by_kind, place, preferred_element_type=F32).astype(BF)
    back_rows = jnp.einsum("ijb,il->jbl", by_kind, place, preferred_element_type=F32).astype(BF)
    fwd_table = rotation_table(kind_pick, fwd_rows, "rotation_table")

    anywhere = pl.BlockSpec(memory_space=pl.ANY)
    halo = whole((2 * NC, TILE, C))
    table_block = pl.BlockSpec((NC, CH, C), lambda s: (0, s, 0))
    scale_block = pl.BlockSpec((CH, C), lambda s: (s, 0))
    weight_scratch = [
        pltpu.VMEM(w_zero.shape, BF),
        pltpu.VMEM(w_one.shape, BF),
        pltpu.VMEM(w_two.shape, BF),
    ]
    gated, grad, keep, send = pl.pallas_call(
        edge_kernel,
        grid=(STEPS,),
        in_specs=[
            pl.BlockSpec(memory_space=pltpu.SMEM),
            table_block,
            pl.BlockSpec((CH, 3 * TILE), lambda s: (s, 0)),
            pl.BlockSpec((CH, 3 * TILE), lambda s: (s, 0)),
            scale_block,
            halo,
            halo,
            halo,
            anywhere,
            anywhere,
            anywhere,
        ],
        out_specs=[anywhere] * 4,
        out_shape=[
            jax.ShapeDtypeStruct((NC, E, C), BF),
            jax.ShapeDtypeStruct((E, W), BF),
            jax.ShapeDtypeStruct((64, CHUNK, C), BF),
            jax.ShapeDtypeStruct((64, CHUNK, C), BF),
        ],
        scratch_shapes=[
            pltpu.VMEM((NC, CH, 2 * C), BF),
            pltpu.VMEM((NC, CH, C), F32),
            pltpu.VMEM((E, W), BF),
            pltpu.VMEM((W, E), BF),
            pltpu.VMEM((E, W), BF),
            pltpu.VMEM((NC, E, C), BF),
            pltpu.VMEM((E, C), F32),
            pltpu.VMEM((E, C), F32),
            pltpu.VMEM((E, C), F32),
            *weight_scratch,
            pltpu.VMEM((6280, C), F32),
            pltpu.VMEM((3208, C), F32),
            pltpu.VMEM((2, 64, AT_TWO, C), BF),
            pltpu.VMEM((2, 64, CHUNK - AT_TWO, C), BF),
            pltpu.SemaphoreType.DMA((9,)),
        ],
        compiler_params=pltpu.CompilerParams(vmem_limit_bytes=VMEM),
        cost_estimate=pl.CostEstimate(
            flops=20_000_000_000, bytes_accessed=40_000_000, transcendentals=0
        ),
        name="edges_and_weight_grads",
    )(
        core.astype(jnp.int32).reshape(1),
        fwd_table,
        src_pick,
        dst_pick,
        scale,
        low,
        own,
        high,
        w_zero,
        w_one,
        w_two,
    )

    other = lax.ppermute(send, "core", [(0, 1), (1, 0)])
    late_pick, _ = lax.optimization_barrier((kind_pick, send))
    back_table = rotation_table(late_pick, back_rows, "rotation_table_back")
    paired = (keep.astype(F32) + other.astype(F32)).astype(BF)
    exchanged = lax.all_to_all(paired, "chip", 0, 0)

    halo_shape = (2 * NC, TILE, C)
    to_low, centre, to_high = pl.pallas_call(
        back_kernel,
        grid=(STEPS,),
        in_specs=[
            table_block,
            scale_block,
            whole((3 * TILE, E)),
            whole((3 * TILE, E)),
            anywhere,
            anywhere,
            anywhere,
            anywhere,
            anywhere,
        ],
        out_specs=[pl.BlockSpec(halo_shape, lambda s: (0, 0, 0))] * 3,
        out_shape=[
            jax.ShapeDtypeStruct(halo_shape, BF),
            jax.ShapeDtypeStruct(halo_shape, F32),
            jax.ShapeDtypeStruct(halo_shape, BF),
        ],
        scratch_shapes=[
            pltpu.VMEM((NC, E, 2 * C), BF),
            pltpu.VMEM((E, W), BF),
            pltpu.VMEM((E, W), BF),
            pltpu.VMEM((E, W), BF),
            *weight_scratch,
            pltpu.SemaphoreType.DMA((5,)),
        ],
        compiler_params=pltpu.CompilerParams(vmem_limit_bytes=VMEM),
        cost_estimate=pl.CostEstimate(
            flops=20_000_000_000, bytes_accessed=40_000_000, transcendentals=0
        ),
        name="edges_back",
    )(back_table, scale, src_put, dst_put, w_zero, w_one, w_two, gated, grad)

    sums = jnp.sum(exchanged.astype(F32), axis=0)
    from_high, from_low, sums = lax.optimization_barrier(
        (shift(to_low, -1), shift(to_high, 1), sums)
    )

    def total(part):
        value = centre[part] + from_high[part].astype(F32) + from_low[part].astype(F32)
        return (own[part].astype(F32) + value).astype(BF).transpose(1, 0, 2)

    updated = total(slice(0, NC))
    grad_coef = total(slice(NC, 2 * NC))
    grad_one = sums[:ROWS_ONE].reshape(-1)
    grad_two = sums[AT_TWO : AT_TWO + ROWS_TWO].reshape(-1)
    grad_zero = sums[AT_ZERO : AT_ZERO + ROWS_ZERO].reshape(-1)
    return (updated, grad_coef, grad_zero, grad_one, grad_two)


def solution(mesh):
    fine = Mesh(mesh.devices.reshape(-1, 2), ("chip", "core"))
    both = ("chip", "core")
    rows3, rows2 = P(both, None, None), P(both, None)
    in_specs = (rows3, rows3, P(), rows2, P(both), P(both), rows2, rows2, rows2, rows2, P(), P(), P())
    out_specs = (rows3, rows3, P(both), P(both), P(both))
    return jax.shard_map(local, mesh=fine, in_specs=in_specs, out_specs=out_specs, check_vma=False)
```

```python
import jax
import jax.numpy as jnp
import numpy as np
from jax import lax
from jax.experimental import pallas as pl
from jax.experimental.pallas import tpu as pltpu
from jax.sharding import Mesh, PartitionSpec as P

BF = jnp.bfloat16
F32 = jnp.float32
NC = 29
C = 128
E = 768
CH = 256
STEPS = E // CH
TILE = 64
W = NC * C
PARTS = (
    (1, 7, 13, 2, 8, 14, 19, 24),
    (0, 3, 9, 15, 20, 25),
    (4, 10, 16, 21, 26),
    (5, 11, 17, 22, 27),
    (6, 12, 18, 23, 28),
)
ROWS_ONE, ROWS_TWO, ROWS_ZERO = 72, 50, 49
AT_TWO, AT_ZERO, CHUNK = 72, 122, 176
TABLE_STEP = 10
VMEM = 62 * 1024 * 1024
COL_PAIRS = tuple((k, min(2, NC - k)) for k in range(0, NC, 2))


def dot(a, b):
    return jnp.dot(a, b, preferred_element_type=F32)


def dot_nt(a, b):
    return lax.dot_general(a, b, (((1,), (1,)), ((), ())), preferred_element_type=F32)


def place_matrix():
    place = np.zeros((NC, C), np.float32)
    for part in PARTS:
        for spot, coef in enumerate(part):
            place[coef, spot * 16 : spot * 16 + 16] = 1.0
    return jnp.asarray(place, BF)


def prepare_kernel(
    first_ref,
    src_tile,
    dst_tile,
    src_slot,
    dst_slot,
    bucket,
    envelope,
    mask,
    src_pick,
    dst_pick,
    src_put,
    dst_put,
    kind_pick,
    scale,
):
    first = first_ref[0]
    window = lax.broadcasted_iota(jnp.int32, (3 * TILE, C), 0)
    kind = lax.broadcasted_iota(jnp.int32, (kind_pick.shape[1], C), 0)
    for k in range(E // C):
        blocks = (2 * k, 2 * k + 1)
        edges = slice(k * C, (k + 1) * C)

        def row(ref):
            return jnp.concatenate([ref[b : b + 1, :] for b in blocks], axis=1)

        for tile, slot, pick, put in (
            (src_tile, src_slot, src_pick, src_put),
            (dst_tile, dst_slot, dst_pick, dst_put),
        ):
            index = jnp.concatenate(
                [slot[b : b + 1, :] + (tile[b] - first) * TILE for b in blocks], axis=1
            )
            hit = jnp.where(window == index, 1.0, 0.0)
            put[:, edges] = hit.astype(BF)
            pick[edges, :] = hit.T.astype(BF)
        kind_pick[edges, :] = jnp.where(kind == row(bucket), 1.0, 0.0).T.astype(BF)
        weight = 0.3 * row(envelope) * row(mask).astype(F32)
        scale[edges, :] = jnp.broadcast_to(weight, (C, C)).T


def table_kernel(pick_ref, rows_ref, out):
    row = lax.broadcasted_iota(jnp.int32, (E, 2 * C), 0)
    lane = lax.broadcasted_iota(jnp.int32, (E, 2 * C), 1)
    keep = jnp.where((row % 16) == (lane % 16), 1.0, 0.0).astype(BF)
    for k in range(0, TABLE_STEP, 2):
        pair = jnp.concatenate([rows_ref[k], rows_ref[k + 1]], axis=1)
        value = dot(pick_ref[...], pair).astype(BF) * keep
        out[k] = value[:, :C]
        out[k + 1] = value[:, C:]


def rotation_table(kind_pick, rows, name):
    kinds = kind_pick.shape[1]
    return pl.pallas_call(
        table_kernel,
        grid=(pl.cdiv(NC, TABLE_STEP),),
        in_specs=[
            whole((E, kinds)),
            pl.BlockSpec((TABLE_STEP, kinds, C), lambda i: (i, 0, 0)),
        ],
        out_specs=pl.BlockSpec((TABLE_STEP, E, C), lambda i: (i, 0, 0)),
        out_shape=jax.ShapeDtypeStruct((NC, E, C), BF),
        cost_estimate=pl.CostEstimate(
            flops=NC * E * C * 1024, bytes_accessed=4 * NC * E * C, transcendentals=0
        ),
        name=name,
    )(kind_pick, rows)


def gather_part(ref, rows, part):
    pieces = [ref[coef, rows, :] for coef in part]
    short = 8 - len(part)
    if short:
        pieces.append(jnp.zeros((16 * short, 256), BF))
    return jnp.concatenate(pieces, axis=0)


def turn_part(table_ref, table_rows, ref, rows, part):
    lhs = jnp.concatenate([table_ref[coef, table_rows, :] for coef in part], axis=0)
    return dot(lhs, gather_part(ref, rows, part))


def edge_kernel(
    core_ref,
    table_ref,
    src_ref,
    dst_ref,
    scale_ref,
    low_ref,
    own_ref,
    high_ref,
    w_zero_hbm,
    w_one_hbm,
    w_two_hbm,
    gated_hbm,
    grad_hbm,
    keep_hbm,
    send_hbm,
    both,
    turned,
    rot,
    rot_t,
    grad,
    gated,
    scalar,
    gate_value,
    first,
    total,
    w_zero,
    w_one,
    w_two,
    flat_one,
    flat_two,
    flat_zero,
    joined,
    stage,
    sems,
):
    step = pl.program_id(0)

    def weight_copy(k):
        source, held = ((w_zero_hbm, w_zero), (w_one_hbm, w_one), (w_two_hbm, w_two))[k]
        return pltpu.make_async_copy(source, held, sems.at[k])

    @pl.when(step == 0)
    def _():
        for k in range(3):
            weight_copy(k).start()
        weight_copy(0).wait()

    for half, picker in ((0, src_ref), (1, dst_ref)):
        for start, width in COL_PAIRS:
            window = [
                jnp.concatenate(
                    [ref[half * NC + k] for ref in (low_ref, own_ref, high_ref)], axis=0
                )
                for k in range(start, start + width)
            ]
            picked = dot(picker[...], jnp.concatenate(window, axis=1)).astype(BF)
            for k in range(width):
                both[start + k, :, half * C : half * C + C] = picked[:, k * C : (k + 1) * C]

    base = pl.multiple_of(step * CH, CH)

    def turn_group(g, carry):
        rows = pl.ds(pl.multiple_of(g * 16, 16), 16)
        out_rows = pl.ds(pl.multiple_of(base + g * 16, 16), 16)
        for part in PARTS:
            out = turn_part(table_ref, rows, both, rows, part)
            for spot, coef in enumerate(part):
                piece = out[spot * 16 : spot * 16 + 16]
                rot[out_rows, coef * C : (coef + 1) * C] = piece[:, :C].astype(BF)
                turned[coef, rows, :] = piece[:, C:]
        return carry

    lax.fori_loop(0, CH // 16, turn_group, 0, unroll=CH // 16)

    here = pl.ds(base, CH)
    t = dot(rot[here, : 7 * C], w_zero[:, :C])
    scalar[here, :] = t
    edge_scale = scale_ref[...]
    first[here, :] = turned[0] * edge_scale
    sig = jax.nn.sigmoid(t)
    gate_value[here, :] = sig
    factor = sig * edge_scale
    for coef in range(1, NC):
        grad[here, coef * C : (coef + 1) * C] = (turned[coef] * factor).astype(BF)
    for coef in range(NC):
        rot_t[coef * C : (coef + 1) * C, here] = rot[here, coef * C : (coef + 1) * C].T

    @pl.when(step == STEPS - 1)
    def _():
        weight_copy(1).wait()
        weight_copy(2).wait()
        total[...] = jnp.zeros_like(total)

        def gate(hidden, coef, count):
            sig = gate_value[...]
            for k in range(count):
                value = hidden[:, k * C : (k + 1) * C]
                gated[coef + k] = (value * sig).astype(BF)
                if not (isinstance(coef, int) and coef + k == 0):
                    lanes = pl.ds(pl.multiple_of((coef + k) * C, C), C)
                    total[...] += value * grad[:, lanes].astype(F32)

        for n in range(4):
            width = 2 if n < 3 else 1
            gate(
                dot(rot[:, : 7 * C], w_zero[:, 2 * n * C : (2 * n + width) * C]), 2 * n, width
            )

        def so_two(weights, begin, half):
            mid = begin + half

            def run(lanes, n, width):
                pair = rot[:, begin * C : (mid + half) * C]
                real, imag = weights[0, :, lanes], weights[1, :, lanes]
                gate(dot(pair, jnp.concatenate([real, -imag], axis=0)), begin + 2 * n, width)
                gate(dot(pair, jnp.concatenate([imag, real], axis=0)), mid + 2 * n, width)

            def body(n, carry):
                run(pl.ds(pl.multiple_of(n * 256, 256), 256), n, 2)
                return carry

            lax.fori_loop(0, half // 2, body, 0)
            if half % 2:
                run(slice((half - 1) * C, half * C), half // 2, 1)

        so_two(w_one, 7, 6)
        so_two(w_two, 19, 5)

        t_all = scalar[...]
        sig = gate_value[...]
        rest = 1.0 - sig
        grad[:, :C] = (first[...] * sig * (1.0 + t_all * rest) + rest * total[...]).astype(BF)

        outs = [
            pltpu.make_async_copy(gated, gated_hbm, sems.at[3]),
            pltpu.make_async_copy(grad, grad_hbm, sems.at[4]),
        ]
        for copy in outs:
            copy.start()

        core = core_ref[0]

        def spread(value, flat, tile, width, tiles):
            rows = value.shape[0]
            for k in range(width):
                flat[pl.ds(tile + k, rows, stride=tiles), :] = value[:, k * C : (k + 1) * C]

        z_t = rot_t[: 7 * C, :]
        for n in range(4):
            width = 2 if n < 3 else 1
            spread(dot(z_t, grad[:, n * 256 : n * 256 + width * C]), flat_zero, 2 * n, width, 7)

        def complex_grad(begin, half, flat, imaginary):
            mid = begin + half
            plus, minus = rot_t[begin * C : mid * C, :], rot_t[mid * C : (mid + half) * C, :]
            both_t = jnp.concatenate([plus, minus], axis=1)
            for n in range((half + 1) // 2):
                width = min(2, half - 2 * n)
                g_p = grad[:, (begin + 2 * n) * C : (begin + 2 * n + width) * C]
                g_m = grad[:, (mid + 2 * n) * C : (mid + 2 * n + width) * C]
                pair = [g_m, -g_p] if imaginary else [g_p, g_m]
                spread(dot(both_t, jnp.concatenate(pair, axis=0)), flat, 2 * n, width, half)

        def pack(first_chip):
            def body(chip, carry):
                for parity in range(2):
                    device = 2 * chip + parity
                    box = joined.at[lax.rem(device, 8)]
                    box[:72, :] = flat_one[pl.ds(pl.multiple_of(device * ROWS_ONE, 8), 72), :]
                    box[72:128, :] = flat_two[pl.ds(device * ROWS_TWO, 56), :]
                    box[AT_ZERO : AT_ZERO + 56, :] = flat_zero[
                        pl.ds((2 * first_chip + device) * ROWS_ZERO, 56), :
                    ]
                    stage[jnp.bitwise_xor(core, parity), first_chip + chip] = box[
                        :CHUNK, :
                    ].astype(BF)
                return carry

            lax.fori_loop(0, 32, body, 0, unroll=8)

        for imaginary in (False, True):
            chips = pl.ds(32 if imaginary else 0, 32)
            complex_grad(7, 6, flat_one, imaginary)
            complex_grad(19, 5, flat_two, imaginary)
            pack(32 if imaginary else 0)
            for slot, target in ((0, keep_hbm), (1, send_hbm)):
                copy = pltpu.make_async_copy(
                    stage.at[slot, chips], target.at[chips], sems.at[5 + 2 * imaginary + slot]
                )
                copy.start()
                outs.append(copy)
        for copy in outs:
            copy.wait()


def back_kernel(
    table_ref,
    scale_ref,
    src_ref,
    dst_ref,
    w_zero_hbm,
    w_one_hbm,
    w_two_hbm,
    gated_hbm,
    grad_hbm,
    low_ref,
    own_ref,
    high_ref,
    both,
    grad,
    message,
    source,
    w_zero,
    w_one,
    w_two,
    sems,
):
    step = pl.program_id(0)

    @pl.when(step == 0)
    def _():
        copies = [
            pltpu.make_async_copy(grad_hbm, grad, sems.at[0]),
            pltpu.make_async_copy(w_zero_hbm, w_zero, sems.at[1]),
            pltpu.make_async_copy(w_one_hbm, w_one, sems.at[2]),
            pltpu.make_async_copy(w_two_hbm, w_two, sems.at[3]),
            pltpu.make_async_copy(gated_hbm, both.at[:, :, :C], sems.at[4]),
        ]
        for copy in copies:
            copy.start()
        copies[0].wait()
        copies[1].wait()

        def put(value, coef, count):
            for k in range(count):
                both[coef + k, :, C:] = value[:, k * C : (k + 1) * C].astype(BF)

        for n in range(4):
            width = 2 if n < 3 else 1
            put(dot_nt(grad[:, : 7 * C], w_zero[2 * n * C : (2 * n + width) * C, :]), 2 * n, width)

        def so_two_back(weights, begin, half):
            mid = begin + half

            def run(rows, n, width):
                pair = grad[:, begin * C : (mid + half) * C]
                real, imag = weights[0, rows, :], weights[1, rows, :]
                put(dot_nt(pair, jnp.concatenate([real, imag], axis=1)), begin + 2 * n, width)
                put(dot_nt(pair, jnp.concatenate([-imag, real], axis=1)), mid + 2 * n, width)

            def body(n, carry):
                run(pl.ds(pl.multiple_of(n * 256, 256), 256), n, 2)
                return carry

            lax.fori_loop(0, half // 2, body, 0)
            if half % 2:
                run(slice((half - 1) * C, half * C), half // 2, 1)

        copies[2].wait()
        so_two_back(w_one, 7, 6)
        copies[3].wait()
        so_two_back(w_two, 19, 5)
        copies[4].wait()

    base = pl.multiple_of(step * CH, CH)

    def turn_group(g, carry):
        rows = pl.ds(pl.multiple_of(g * 16, 16), 16)
        out_rows = pl.ds(pl.multiple_of(base + g * 16, 16), 16)
        edge_scale = scale_ref[rows, :]
        for part in PARTS:
            out = turn_part(table_ref, rows, both, out_rows, part)
            for spot, coef in enumerate(part):
                piece = out[spot * 16 : spot * 16 + 16]
                lanes = slice(coef * C, (coef + 1) * C)
                message[out_rows, lanes] = (piece[:, :C] * edge_scale).astype(BF)
                source[out_rows, lanes] = piece[:, C:].astype(BF)
        return carry

    lax.fori_loop(0, CH // 16, turn_group, 0, unroll=CH // 16)

    @pl.when(step == STEPS - 1)
    def _():
        for half, picker, values in ((0, dst_ref, message), (1, src_ref, source)):
            for start, width in COL_PAIRS:
                summed = dot(picker[...], values[:, start * C : (start + width) * C])
                for k in range(width):
                    at = half * NC + start + k
                    piece = summed[:, k * C : (k + 1) * C]
                    low_ref[at] = piece[:TILE].astype(BF)
                    own_ref[at] = piece[TILE : 2 * TILE]
                    high_ref[at] = piece[2 * TILE :].astype(BF)


def whole(shape):
    return pl.BlockSpec(shape, lambda *_: (0,) * len(shape), pipeline_mode=pl.Buffered(1))


def shift(value, steps):
    count = lax.axis_size("chip") * 2
    pairs = [(i, i + steps) for i in range(count) if 0 <= i + steps < count]
    return lax.ppermute(value, ("chip", "core"), pairs)


def local(
    node_coef,
    cotangent,
    wigner,
    envelope,
    src_tile,
    dst_tile,
    src_slot,
    dst_slot,
    bucket,
    mask,
    w_zero,
    w_one,
    w_two,
):
    core = lax.axis_index("core")
    device = lax.axis_index("chip") * 2 + core
    own = jnp.concatenate(
        [node_coef.transpose(1, 0, 2), cotangent.transpose(1, 0, 2)], axis=0
    )
    low = shift(own, 1)
    high = shift(own, -1)

    kinds = wigner.shape[0]
    smem = pl.BlockSpec(memory_space=pltpu.SMEM)
    vmem = pl.BlockSpec(memory_space=pltpu.VMEM)
    src_pick, dst_pick, src_put, dst_put, kind_pick, scale = pl.pallas_call(
        prepare_kernel,
        in_specs=[smem, smem, smem, vmem, vmem, vmem, vmem, vmem],
        out_specs=[vmem] * 6,
        out_shape=[
            jax.ShapeDtypeStruct((E, 3 * TILE), BF),
            jax.ShapeDtypeStruct((E, 3 * TILE), BF),
            jax.ShapeDtypeStruct((3 * TILE, E), BF),
            jax.ShapeDtypeStruct((3 * TILE, E), BF),
            jax.ShapeDtypeStruct((E, kinds), BF),
            jax.ShapeDtypeStruct((E, C), F32),
        ],
        name="prepare",
    )(
        (device - 1).astype(jnp.int32).reshape(1),
        src_tile,
        dst_tile,
        src_slot,
        dst_slot,
        bucket,
        envelope,
        mask,
    )

    place = place_matrix()
    by_kind = wigner.transpose(1, 2, 0)
    fwd_rows = jnp.einsum("ijb,jl->ibl", by_kind, place, preferred_element_type=F32).astype(BF)
    back_rows = jnp.einsum("ijb,il->jbl", by_kind, place, preferred_element_type=F32).astype(BF)
    fwd_table = rotation_table(kind_pick, fwd_rows, "rotation_table")

    anywhere = pl.BlockSpec(memory_space=pl.ANY)
    halo = whole((2 * NC, TILE, C))
    table_block = pl.BlockSpec((NC, CH, C), lambda s: (0, s, 0))
    scale_block = pl.BlockSpec((CH, C), lambda s: (s, 0))
    weight_scratch = [
        pltpu.VMEM(w_zero.shape, BF),
        pltpu.VMEM(w_one.shape, BF),
        pltpu.VMEM(w_two.shape, BF),
    ]
    gated, grad, keep, send = pl.pallas_call(
        edge_kernel,
        grid=(STEPS,),
        in_specs=[
            pl.BlockSpec(memory_space=pltpu.SMEM),
            table_block,
            pl.BlockSpec((CH, 3 * TILE), lambda s: (s, 0)),
            pl.BlockSpec((CH, 3 * TILE), lambda s: (s, 0)),
            scale_block,
            halo,
            halo,
            halo,
            anywhere,
            anywhere,
            anywhere,
        ],
        out_specs=[anywhere] * 4,
        out_shape=[
            jax.ShapeDtypeStruct((NC, E, C), BF),
            jax.ShapeDtypeStruct((E, W), BF),
            jax.ShapeDtypeStruct((64, CHUNK, C), BF),
            jax.ShapeDtypeStruct((64, CHUNK, C), BF),
        ],
        scratch_shapes=[
            pltpu.VMEM((NC, CH, 2 * C), BF),
            pltpu.VMEM((NC, CH, C), F32),
            pltpu.VMEM((E, W), BF),
            pltpu.VMEM((W, E), BF),
            pltpu.VMEM((E, W), BF),
            pltpu.VMEM((NC, E, C), BF),
            pltpu.VMEM((E, C), F32),
            pltpu.VMEM((E, C), F32),
            pltpu.VMEM((E, C), F32),
            pltpu.VMEM((E, C), F32),
            *weight_scratch,
            pltpu.VMEM((4616, C), F32),
            pltpu.VMEM((3208, C), F32),
            pltpu.VMEM((6280, C), F32),
            pltpu.VMEM((8, 184, C), F32),
            pltpu.VMEM((2, 64, CHUNK, C), BF),
            pltpu.SemaphoreType.DMA((9,)),
        ],
        compiler_params=pltpu.CompilerParams(vmem_limit_bytes=VMEM),
        cost_estimate=pl.CostEstimate(
            flops=20_000_000_000, bytes_accessed=40_000_000, transcendentals=0
        ),
        name="edges_and_weight_grads",
    )(
        core.astype(jnp.int32).reshape(1),
        fwd_table,
        src_pick,
        dst_pick,
        scale,
        low,
        own,
        high,
        w_zero,
        w_one,
        w_two,
    )

    other = lax.ppermute(send, "core", [(0, 1), (1, 0)])
    late_pick, _ = lax.optimization_barrier((kind_pick, send))
    back_table = rotation_table(late_pick, back_rows, "rotation_table_back")
    keep, back_table = lax.optimization_barrier((keep, back_table))
    paired = keep + other
    exchanged = lax.all_to_all(paired, "chip", 0, 0)

    halo_shape = (2 * NC, TILE, C)
    to_low, centre, to_high = pl.pallas_call(
        back_kernel,
        grid=(STEPS,),
        in_specs=[
            table_block,
            scale_block,
            whole((3 * TILE, E)),
            whole((3 * TILE, E)),
            anywhere,
            anywhere,
            anywhere,
            anywhere,
            anywhere,
        ],
        out_specs=[pl.BlockSpec(halo_shape, lambda s: (0, 0, 0))] * 3,
        out_shape=[
            jax.ShapeDtypeStruct(halo_shape, BF),
            jax.ShapeDtypeStruct(halo_shape, F32),
            jax.ShapeDtypeStruct(halo_shape, BF),
        ],
        scratch_shapes=[
            pltpu.VMEM((NC, E, 2 * C), BF),
            pltpu.VMEM((E, W), BF),
            pltpu.VMEM((E, W), BF),
            pltpu.VMEM((E, W), BF),
            *weight_scratch,
            pltpu.SemaphoreType.DMA((5,)),
        ],
        compiler_params=pltpu.CompilerParams(vmem_limit_bytes=VMEM),
        cost_estimate=pl.CostEstimate(
            flops=20_000_000_000, bytes_accessed=40_000_000, transcendentals=0
        ),
        name="edges_back",
    )(back_table, scale, src_put, dst_put, w_zero, w_one, w_two, gated, grad)

    sums = jnp.sum(exchanged.astype(F32), axis=0)
    grad_one = sums[:ROWS_ONE].reshape(-1)
    grad_two = sums[AT_TWO : AT_TWO + ROWS_TWO].reshape(-1)
    grad_zero = sums[AT_ZERO : AT_ZERO + ROWS_ZERO].reshape(-1)
    from_high, from_low, grad_zero, grad_one, grad_two = lax.optimization_barrier(
        (shift(to_low, -1), shift(to_high, 1), grad_zero, grad_one, grad_two)
    )

    def total(part):
        value = centre[part] + from_high[part].astype(F32) + from_low[part].astype(F32)
        return (own[part].astype(F32) + value).astype(BF).transpose(1, 0, 2)

    updated = total(slice(0, NC))
    grad_coef = total(slice(NC, 2 * NC))
    return (updated, grad_coef, grad_zero, grad_one, grad_two)


def solution(mesh):
    fine = Mesh(mesh.devices.reshape(-1, 2), ("chip", "core"))
    both = ("chip", "core")
    rows3, rows2 = P(both, None, None), P(both, None)
    in_specs = (rows3, rows3, P(), rows2, P(both), P(both), rows2, rows2, rows2, rows2, P(), P(), P())
    out_specs = (rows3, rows3, P(both), P(both), P(both))
    return jax.shard_map(local, mesh=fine, in_specs=in_specs, out_specs=out_specs, check_vma=False)
```

```python
import jax
import jax.numpy as jnp
import numpy as np
from jax import lax
from jax.experimental import pallas as pl
from jax.experimental.pallas import tpu as pltpu
from jax.sharding import Mesh, PartitionSpec as P

BF = jnp.bfloat16
F32 = jnp.float32
NC = 29
C = 128
E = 768
CH = 256
STEPS = E // CH
TILE = 64
W = NC * C
PARTS = (
    (1, 7, 13, 2, 8, 14, 19, 24),
    (0, 3, 9, 15, 20, 25),
    (4, 10, 16, 21, 26),
    (5, 11, 17, 22, 27),
    (6, 12, 18, 23, 28),
)
ROWS_ONE, ROWS_TWO, ROWS_ZERO = 72, 50, 49
AT_TWO, AT_ZERO, CHUNK = 72, 122, 176
TABLE_STEP = 10
VMEM = 62 * 1024 * 1024
COL_PAIRS = tuple((k, min(2, NC - k)) for k in range(0, NC, 2))


def dot(a, b):
    return jnp.dot(a, b, preferred_element_type=F32)


def dot_nt(a, b):
    return lax.dot_general(a, b, (((1,), (1,)), ((), ())), preferred_element_type=F32)


def place_matrix():
    place = np.zeros((NC, C), np.float32)
    for part in PARTS:
        for spot, coef in enumerate(part):
            place[coef, spot * 16 : spot * 16 + 16] = 1.0
    return jnp.asarray(place, BF)


def prepare_kernel(
    first_ref,
    src_tile,
    dst_tile,
    src_slot,
    dst_slot,
    bucket,
    envelope,
    mask,
    src_pick,
    dst_pick,
    src_put,
    dst_put,
    kind_pick,
    scale,
):
    first = first_ref[0]
    window = lax.broadcasted_iota(jnp.int32, (3 * TILE, C), 0)
    kind = lax.broadcasted_iota(jnp.int32, (kind_pick.shape[1], C), 0)
    for k in range(E // C):
        blocks = (2 * k, 2 * k + 1)
        edges = slice(k * C, (k + 1) * C)

        def row(ref):
            return jnp.concatenate([ref[b : b + 1, :] for b in blocks], axis=1)

        for tile, slot, pick, put in (
            (src_tile, src_slot, src_pick, src_put),
            (dst_tile, dst_slot, dst_pick, dst_put),
        ):
            index = jnp.concatenate(
                [slot[b : b + 1, :] + (tile[b] - first) * TILE for b in blocks], axis=1
            )
            hit = jnp.where(window == index, 1.0, 0.0)
            put[:, edges] = hit.astype(BF)
            pick[edges, :] = hit.T.astype(BF)
        kind_pick[edges, :] = jnp.where(kind == row(bucket), 1.0, 0.0).T.astype(BF)
        weight = 0.3 * row(envelope) * row(mask).astype(F32)
        scale[edges, :] = jnp.broadcast_to(weight, (C, C)).T


def table_kernel(pick_ref, rows_ref, out):
    row = lax.broadcasted_iota(jnp.int32, (E, 2 * C), 0)
    lane = lax.broadcasted_iota(jnp.int32, (E, 2 * C), 1)
    keep = jnp.where((row % 16) == (lane % 16), 1.0, 0.0).astype(BF)
    for k in range(0, TABLE_STEP, 2):
        pair = jnp.concatenate([rows_ref[k], rows_ref[k + 1]], axis=1)
        value = dot(pick_ref[...], pair).astype(BF) * keep
        out[k] = value[:, :C]
        out[k + 1] = value[:, C:]


def rotation_table(kind_pick, rows, name):
    kinds = kind_pick.shape[1]
    return pl.pallas_call(
        table_kernel,
        grid=(pl.cdiv(NC, TABLE_STEP),),
        in_specs=[
            whole((E, kinds)),
            pl.BlockSpec((TABLE_STEP, kinds, C), lambda i: (i, 0, 0)),
        ],
        out_specs=pl.BlockSpec((TABLE_STEP, E, C), lambda i: (i, 0, 0)),
        out_shape=jax.ShapeDtypeStruct((NC, E, C), BF),
        cost_estimate=pl.CostEstimate(
            flops=NC * E * C * 1024, bytes_accessed=4 * NC * E * C, transcendentals=0
        ),
        name=name,
    )(kind_pick, rows)


def gather_part(ref, rows, part):
    pieces = [ref[coef, rows, :] for coef in part]
    short = 8 - len(part)
    if short:
        pieces.append(jnp.zeros((16 * short, 256), BF))
    return jnp.concatenate(pieces, axis=0)


def turn_part(table_ref, table_rows, ref, rows, part):
    lhs = jnp.concatenate([table_ref[coef, table_rows, :] for coef in part], axis=0)
    return dot(lhs, gather_part(ref, rows, part))


def edge_kernel(
    core_ref,
    table_ref,
    src_ref,
    dst_ref,
    scale_ref,
    low_ref,
    own_ref,
    high_ref,
    w_zero_hbm,
    w_one_hbm,
    w_two_hbm,
    gated_hbm,
    grad_hbm,
    keep_hbm,
    send_hbm,
    both,
    turned,
    rot,
    rot_t,
    grad,
    gated,
    scalar,
    gate_value,
    first,
    total,
    w_zero,
    w_one,
    w_two,
    flat_one,
    flat_two,
    flat_zero,
    joined,
    stage,
    sems,
):
    step = pl.program_id(0)

    def weight_copy(k):
        source, held = ((w_zero_hbm, w_zero), (w_one_hbm, w_one), (w_two_hbm, w_two))[k]
        return pltpu.make_async_copy(source, held, sems.at[k])

    @pl.when(step == 0)
    def _():
        for k in range(3):
            weight_copy(k).start()

    for half, picker in ((0, src_ref), (1, dst_ref)):
        for start, width in COL_PAIRS:
            window = [
                jnp.concatenate(
                    [ref[half * NC + k] for ref in (low_ref, own_ref, high_ref)], axis=0
                )
                for k in range(start, start + width)
            ]
            picked = dot(picker[...], jnp.concatenate(window, axis=1)).astype(BF)
            for k in range(width):
                both[start + k, :, half * C : half * C + C] = picked[:, k * C : (k + 1) * C]

    base = pl.multiple_of(step * CH, CH)

    def turn_group(g, carry):
        rows = pl.ds(pl.multiple_of(g * 16, 16), 16)
        out_rows = pl.ds(pl.multiple_of(base + g * 16, 16), 16)
        for part in PARTS:
            out = turn_part(table_ref, rows, both, rows, part)
            for spot, coef in enumerate(part):
                piece = out[spot * 16 : spot * 16 + 16]
                rot[out_rows, coef * C : (coef + 1) * C] = piece[:, :C].astype(BF)
                turned[coef, rows, :] = piece[:, C:]
        return carry

    lax.fori_loop(0, CH // 16, turn_group, 0, unroll=CH // 16)

    @pl.when(step == 0)
    def _():
        weight_copy(0).wait()

    here = pl.ds(base, CH)
    t = dot(rot[here, : 7 * C], w_zero[:, :C])
    scalar[here, :] = t
    edge_scale = scale_ref[...]
    first[here, :] = turned[0] * edge_scale
    sig = jax.nn.sigmoid(t)
    gate_value[here, :] = sig
    factor = sig * edge_scale
    for coef in range(1, NC):
        grad[here, coef * C : (coef + 1) * C] = (turned[coef] * factor).astype(BF)
    for coef in range(NC):
        rot_t[coef * C : (coef + 1) * C, here] = rot[here, coef * C : (coef + 1) * C].T

    @pl.when(step == STEPS - 1)
    def _():
        weight_copy(1).wait()
        weight_copy(2).wait()
        total[...] = jnp.zeros_like(total)

        def gate(hidden, coef, count):
            sig = gate_value[...]
            for k in range(count):
                value = hidden[:, k * C : (k + 1) * C]
                gated[coef + k] = (value * sig).astype(BF)
                if coef + k:
                    lanes = slice((coef + k) * C, (coef + k + 1) * C)
                    total[...] += value * grad[:, lanes].astype(F32)

        for n in range(4):
            width = 2 if n < 3 else 1
            gate(
                dot(rot[:, : 7 * C], w_zero[:, 2 * n * C : (2 * n + width) * C]), 2 * n, width
            )

        def so_two(weights, begin, half):
            mid = begin + half

            def run(lanes, n, width):
                pair = rot[:, begin * C : (mid + half) * C]
                real, imag = weights[0, :, lanes], weights[1, :, lanes]
                gate(dot(pair, jnp.concatenate([real, -imag], axis=0)), begin + 2 * n, width)
                gate(dot(pair, jnp.concatenate([imag, real], axis=0)), mid + 2 * n, width)

            for n in range(half // 2):
                run(slice(n * 256, (n + 1) * 256), n, 2)
            if half % 2:
                pair = rot[:, begin * C : (mid + half) * C]
                lanes = slice((half - 1) * C, half * C)
                real, imag = weights[0, :, lanes], weights[1, :, lanes]
                upper = jnp.concatenate([real, imag], axis=1)
                lower = jnp.concatenate([-imag, real], axis=1)
                value = dot(pair, jnp.concatenate([upper, lower], axis=0))
                gate(value[:, :C], mid - 1, 1)
                gate(value[:, C:], mid + half - 1, 1)

        so_two(w_one, 7, 6)
        so_two(w_two, 19, 5)

        t_all = scalar[...]
        sig = gate_value[...]
        rest = 1.0 - sig
        grad[:, :C] = (first[...] * sig * (1.0 + t_all * rest) + rest * total[...]).astype(BF)

        outs = [
            pltpu.make_async_copy(gated, gated_hbm, sems.at[3]),
            pltpu.make_async_copy(grad, grad_hbm, sems.at[4]),
        ]
        for copy in outs:
            copy.start()

        core = core_ref[0]

        def spread(value, flat, tile, width, tiles):
            rows = value.shape[0]
            for k in range(width):
                flat[pl.ds(tile + k, rows, stride=tiles), :] = value[:, k * C : (k + 1) * C]

        z_t = rot_t[: 7 * C, :]
        for n in range(4):
            width = 2 if n < 3 else 1
            spread(dot(z_t, grad[:, n * 256 : n * 256 + width * C]), flat_zero, 2 * n, width, 7)

        def complex_grad(begin, half, flat, imaginary):
            mid = begin + half
            plus, minus = rot_t[begin * C : mid * C, :], rot_t[mid * C : (mid + half) * C, :]
            both_t = jnp.concatenate([plus, minus], axis=1)
            for n in range((half + 1) // 2):
                width = min(2, half - 2 * n)
                g_p = grad[:, (begin + 2 * n) * C : (begin + 2 * n + width) * C]
                g_m = grad[:, (mid + 2 * n) * C : (mid + 2 * n + width) * C]
                pair = [g_m, -g_p] if imaginary else [g_p, g_m]
                spread(dot(both_t, jnp.concatenate(pair, axis=0)), flat, 2 * n, width, half)

        def pack(first_chip):
            def body(chip, carry):
                for parity in range(2):
                    device = 2 * chip + parity
                    box = joined.at[lax.rem(device, 8)]
                    box[:72, :] = flat_one[pl.ds(pl.multiple_of(device * ROWS_ONE, 8), 72), :]
                    box[72:128, :] = flat_two[pl.ds(device * ROWS_TWO, 56), :]
                    box[AT_ZERO : AT_ZERO + 56, :] = flat_zero[
                        pl.ds((2 * first_chip + device) * ROWS_ZERO, 56), :
                    ]
                    stage[jnp.bitwise_xor(core, parity), first_chip + chip] = box[
                        :CHUNK, :
                    ].astype(BF)
                return carry

            lax.fori_loop(0, 32, body, 0, unroll=8)

        for imaginary in (False, True):
            chips = pl.ds(32 if imaginary else 0, 32)
            complex_grad(7, 6, flat_one, imaginary)
            complex_grad(19, 5, flat_two, imaginary)
            pack(32 if imaginary else 0)
            for slot, target in ((0, keep_hbm), (1, send_hbm)):
                copy = pltpu.make_async_copy(
                    stage.at[slot, chips], target.at[chips], sems.at[5 + 2 * imaginary + slot]
                )
                copy.start()
                outs.append(copy)
        for copy in outs:
            copy.wait()


def back_kernel(
    table_ref,
    scale_ref,
    src_ref,
    dst_ref,
    w_zero_hbm,
    w_one_hbm,
    w_two_hbm,
    gated_hbm,
    grad_hbm,
    low_hbm,
    own_hbm,
    high_hbm,
    low_ref,
    own_ref,
    high_ref,
    both,
    grad,
    message,
    source,
    w_zero,
    w_one,
    w_two,
    sems,
):
    step = pl.program_id(0)

    @pl.when(step == 0)
    def _():
        copies = []
        for k, (lanes, source, held) in enumerate(
            (
                (slice(0, 7 * C), w_zero_hbm, w_zero),
                (slice(7 * C, 19 * C), w_one_hbm, w_one),
                (slice(19 * C, W), w_two_hbm, w_two),
            )
        ):
            copies.append(
                (
                    pltpu.make_async_copy(source, held, sems.at[2 * k]),
                    pltpu.make_async_copy(
                        grad_hbm.at[:, lanes], grad.at[:, lanes], sems.at[2 * k + 1]
                    ),
                )
            )
        copies.append((pltpu.make_async_copy(gated_hbm, both.at[:, :, :C], sems.at[6]),))
        for group in copies:
            for copy in group:
                copy.start()

        def arrive(k):
            for copy in copies[k]:
                copy.wait()

        arrive(0)

        def put(value, coef, count):
            for k in range(count):
                both[coef + k, :, C:] = value[:, k * C : (k + 1) * C].astype(BF)

        for n in range(4):
            width = 2 if n < 3 else 1
            put(dot_nt(grad[:, : 7 * C], w_zero[2 * n * C : (2 * n + width) * C, :]), 2 * n, width)

        def so_two_back(weights, begin, half):
            mid = begin + half

            def run(rows, n, width):
                pair = grad[:, begin * C : (mid + half) * C]
                real, imag = weights[0, rows, :], weights[1, rows, :]
                put(dot_nt(pair, jnp.concatenate([real, imag], axis=1)), begin + 2 * n, width)
                put(dot_nt(pair, jnp.concatenate([-imag, real], axis=1)), mid + 2 * n, width)

            for n in range(half // 2):
                run(slice(n * 256, (n + 1) * 256), n, 2)
            if half % 2:
                pair = grad[:, begin * C : (mid + half) * C]
                rows = slice((half - 1) * C, half * C)
                real, imag = weights[0, rows, :], weights[1, rows, :]
                upper = jnp.concatenate([real, imag], axis=1)
                lower = jnp.concatenate([-imag, real], axis=1)
                value = dot_nt(pair, jnp.concatenate([upper, lower], axis=0))
                put(value[:, :C], mid - 1, 1)
                put(value[:, C:], mid + half - 1, 1)

        arrive(1)
        so_two_back(w_one, 7, 6)
        arrive(2)
        so_two_back(w_two, 19, 5)
        arrive(3)

    base = pl.multiple_of(step * CH, CH)

    def turn_group(g, carry):
        rows = pl.ds(pl.multiple_of(g * 16, 16), 16)
        out_rows = pl.ds(pl.multiple_of(base + g * 16, 16), 16)
        edge_scale = scale_ref[rows, :]
        for part in PARTS:
            out = turn_part(table_ref, rows, both, out_rows, part)
            for spot, coef in enumerate(part):
                piece = out[spot * 16 : spot * 16 + 16]
                lanes = slice(coef * C, (coef + 1) * C)
                message[out_rows, lanes] = (piece[:, :C] * edge_scale).astype(BF)
                source[out_rows, lanes] = piece[:, C:].astype(BF)
        return carry

    lax.fori_loop(0, CH // 16, turn_group, 0, unroll=CH // 16)

    @pl.when(step == STEPS - 1)
    def _():
        outs = []
        for half, picker, values in ((0, dst_ref, message), (1, src_ref, source)):
            for start, width in COL_PAIRS:
                summed = dot(picker[...], values[:, start * C : (start + width) * C])
                for k in range(width):
                    at = half * NC + start + k
                    piece = summed[:, k * C : (k + 1) * C]
                    low_ref[at] = piece[:TILE].astype(BF)
                    own_ref[at] = piece[TILE : 2 * TILE]
                    high_ref[at] = piece[2 * TILE :].astype(BF)
            kept = slice(half * NC, (half + 1) * NC)
            for k, (held, target) in enumerate(
                ((low_ref, low_hbm), (high_ref, high_hbm), (own_ref, own_hbm))
            ):
                copy = pltpu.make_async_copy(
                    held.at[kept], target.at[kept], sems.at[7 + 3 * half + k]
                )
                copy.start()
                outs.append(copy)
        for copy in outs:
            copy.wait()


def whole(shape):
    return pl.BlockSpec(shape, lambda *_: (0,) * len(shape), pipeline_mode=pl.Buffered(1))


def shift(value, steps):
    count = lax.axis_size("chip") * 2
    pairs = [(i, i + steps) for i in range(count) if 0 <= i + steps < count]
    return lax.ppermute(value, ("chip", "core"), pairs)


def local(
    node_coef,
    cotangent,
    wigner,
    envelope,
    src_tile,
    dst_tile,
    src_slot,
    dst_slot,
    bucket,
    mask,
    w_zero,
    w_one,
    w_two,
):
    core = lax.axis_index("core")
    device = lax.axis_index("chip") * 2 + core
    own = jnp.concatenate(
        [node_coef.transpose(1, 0, 2), cotangent.transpose(1, 0, 2)], axis=0
    )
    low = shift(own, 1)
    high = shift(own, -1)

    kinds = wigner.shape[0]
    smem = pl.BlockSpec(memory_space=pltpu.SMEM)
    vmem = pl.BlockSpec(memory_space=pltpu.VMEM)
    src_pick, dst_pick, src_put, dst_put, kind_pick, scale = pl.pallas_call(
        prepare_kernel,
        in_specs=[smem, smem, smem, vmem, vmem, vmem, vmem, vmem],
        out_specs=[vmem] * 6,
        out_shape=[
            jax.ShapeDtypeStruct((E, 3 * TILE), BF),
            jax.ShapeDtypeStruct((E, 3 * TILE), BF),
            jax.ShapeDtypeStruct((3 * TILE, E), BF),
            jax.ShapeDtypeStruct((3 * TILE, E), BF),
            jax.ShapeDtypeStruct((E, kinds), BF),
            jax.ShapeDtypeStruct((E, C), F32),
        ],
        name="prepare",
    )(
        (device - 1).astype(jnp.int32).reshape(1),
        src_tile,
        dst_tile,
        src_slot,
        dst_slot,
        bucket,
        envelope,
        mask,
    )

    place = place_matrix()
    by_kind = wigner.transpose(1, 2, 0)
    fwd_rows = jnp.einsum("ijb,jl->ibl", by_kind, place, preferred_element_type=F32).astype(BF)
    back_rows = jnp.einsum("ijb,il->jbl", by_kind, place, preferred_element_type=F32).astype(BF)
    fwd_table = rotation_table(kind_pick, fwd_rows, "rotation_table")

    anywhere = pl.BlockSpec(memory_space=pl.ANY)
    halo = whole((2 * NC, TILE, C))
    table_block = pl.BlockSpec((NC, CH, C), lambda s: (0, s, 0))
    scale_block = pl.BlockSpec((CH, C), lambda s: (s, 0))
    weight_scratch = [
        pltpu.VMEM(w_zero.shape, BF),
        pltpu.VMEM(w_one.shape, BF),
        pltpu.VMEM(w_two.shape, BF),
    ]
    gated, grad, keep, send = pl.pallas_call(
        edge_kernel,
        grid=(STEPS,),
        in_specs=[
            pl.BlockSpec(memory_space=pltpu.SMEM),
            table_block,
            pl.BlockSpec((CH, 3 * TILE), lambda s: (s, 0)),
            pl.BlockSpec((CH, 3 * TILE), lambda s: (s, 0)),
            scale_block,
            halo,
            halo,
            halo,
            anywhere,
            anywhere,
            anywhere,
        ],
        out_specs=[anywhere] * 4,
        out_shape=[
            jax.ShapeDtypeStruct((NC, E, C), BF),
            jax.ShapeDtypeStruct((E, W), BF),
            jax.ShapeDtypeStruct((64, CHUNK, C), BF),
            jax.ShapeDtypeStruct((64, CHUNK, C), BF),
        ],
        scratch_shapes=[
            pltpu.VMEM((NC, CH, 2 * C), BF),
            pltpu.VMEM((NC, CH, C), F32),
            pltpu.VMEM((E, W), BF),
            pltpu.VMEM((W, E), BF),
            pltpu.VMEM((E, W), BF),
            pltpu.VMEM((NC, E, C), BF),
            pltpu.VMEM((E, C), F32),
            pltpu.VMEM((E, C), F32),
            pltpu.VMEM((E, C), F32),
            pltpu.VMEM((E, C), F32),
            *weight_scratch,
            pltpu.VMEM((4616, C), F32),
            pltpu.VMEM((3208, C), F32),
            pltpu.VMEM((6280, C), F32),
            pltpu.VMEM((8, 184, C), F32),
            pltpu.VMEM((2, 64, CHUNK, C), BF),
            pltpu.SemaphoreType.DMA((9,)),
        ],
        compiler_params=pltpu.CompilerParams(vmem_limit_bytes=VMEM),
        cost_estimate=pl.CostEstimate(
            flops=20_000_000_000, bytes_accessed=40_000_000, transcendentals=0
        ),
        name="edges_and_weight_grads",
    )(
        core.astype(jnp.int32).reshape(1),
        fwd_table,
        src_pick,
        dst_pick,
        scale,
        low,
        own,
        high,
        w_zero,
        w_one,
        w_two,
    )

    other = lax.ppermute(send, "core", [(0, 1), (1, 0)])
    late_pick, _ = lax.optimization_barrier((kind_pick, send))
    back_table = rotation_table(late_pick, back_rows, "rotation_table_back")
    keep, back_table = lax.optimization_barrier((keep, back_table))
    paired = keep + other
    exchanged = lax.all_to_all(paired, "chip", 0, 0)

    halo_shape = (2 * NC, TILE, C)
    to_low, centre, to_high = pl.pallas_call(
        back_kernel,
        grid=(STEPS,),
        in_specs=[
            table_block,
            scale_block,
            whole((3 * TILE, E)),
            whole((3 * TILE, E)),
            anywhere,
            anywhere,
            anywhere,
            anywhere,
            anywhere,
        ],
        out_specs=[anywhere] * 3,
        out_shape=[
            jax.ShapeDtypeStruct(halo_shape, BF),
            jax.ShapeDtypeStruct(halo_shape, F32),
            jax.ShapeDtypeStruct(halo_shape, BF),
        ],
        scratch_shapes=[
            pltpu.VMEM(halo_shape, BF),
            pltpu.VMEM(halo_shape, F32),
            pltpu.VMEM(halo_shape, BF),
            pltpu.VMEM((NC, E, 2 * C), BF),
            pltpu.VMEM((E, W), BF),
            pltpu.VMEM((E, W), BF),
            pltpu.VMEM((E, W), BF),
            *weight_scratch,
            pltpu.SemaphoreType.DMA((13,)),
        ],
        compiler_params=pltpu.CompilerParams(vmem_limit_bytes=VMEM),
        cost_estimate=pl.CostEstimate(
            flops=20_000_000_000, bytes_accessed=40_000_000, transcendentals=0
        ),
        name="edges_back",
    )(back_table, scale, src_put, dst_put, w_zero, w_one, w_two, gated, grad)

    sums = jnp.sum(exchanged.astype(F32), axis=0)
    grad_one = sums[:ROWS_ONE].reshape(-1)
    grad_two = sums[AT_TWO : AT_TWO + ROWS_TWO].reshape(-1)
    grad_zero = sums[AT_ZERO : AT_ZERO + ROWS_ZERO].reshape(-1)
    from_high, from_low, grad_zero, grad_one, grad_two = lax.optimization_barrier(
        (shift(to_low, -1), shift(to_high, 1), grad_zero, grad_one, grad_two)
    )

    def total(part):
        value = centre[part] + from_high[part].astype(F32) + from_low[part].astype(F32)
        return (own[part].astype(F32) + value).astype(BF).transpose(1, 0, 2)

    updated = total(slice(0, NC))
    grad_coef = total(slice(NC, 2 * NC))
    return (updated, grad_coef, grad_zero, grad_one, grad_two)


def solution(mesh):
    fine = Mesh(mesh.devices.reshape(-1, 2), ("chip", "core"))
    both = ("chip", "core")
    rows3, rows2 = P(both, None, None), P(both, None)
    in_specs = (rows3, rows3, P(), rows2, P(both), P(both), rows2, rows2, rows2, rows2, P(), P(), P())
    out_specs = (rows3, rows3, P(both), P(both), P(both))
    return jax.shard_map(local, mesh=fine, in_specs=in_specs, out_specs=out_specs, check_vma=False)
```

```python
import jax
import jax.numpy as jnp
import numpy as np
from jax import lax
from jax.experimental import pallas as pl
from jax.experimental.pallas import tpu as pltpu
from jax.sharding import Mesh, PartitionSpec as P

BF = jnp.bfloat16
F32 = jnp.float32
NC = 29
C = 128
E = 768
CH = 256
STEPS = E // CH
TILE = 64
W = NC * C
PARTS = (
    (1, 7, 13, 2, 8, 14, 19, 24),
    (0, 3, 9, 15, 20, 25),
    (4, 10, 16, 21, 26),
    (5, 11, 17, 22, 27),
    (6, 12, 18, 23, 28),
)
ROWS_ONE, ROWS_TWO, ROWS_ZERO = 72, 50, 49
AT_TWO, AT_ZERO, CHUNK = 72, 122, 176
TABLE_STEP = 10
PIECE = 256
VMEM = 62 * 1024 * 1024
COL_PAIRS = tuple((k, min(2, NC - k)) for k in range(0, NC, 2))


def dot(a, b):
    return jnp.dot(a, b, preferred_element_type=F32)


def dot_nt(a, b):
    return lax.dot_general(a, b, (((1,), (1,)), ((), ())), preferred_element_type=F32)


def place_matrix():
    place = np.zeros((NC, C), np.float32)
    for part in PARTS:
        for spot, coef in enumerate(part):
            place[coef, spot * 16 : spot * 16 + 16] = 1.0
    return jnp.asarray(place, BF)


def prepare_kernel(
    first_ref,
    src_tile,
    dst_tile,
    src_slot,
    dst_slot,
    bucket,
    envelope,
    mask,
    src_pick,
    dst_pick,
    src_put,
    dst_put,
    kind_pick,
    scale,
):
    first = first_ref[0]
    window = lax.broadcasted_iota(jnp.int32, (3 * TILE, C), 0)
    kind = lax.broadcasted_iota(jnp.int32, (kind_pick.shape[1], C), 0)
    for k in range(E // C):
        blocks = (2 * k, 2 * k + 1)
        edges = slice(k * C, (k + 1) * C)

        def row(ref):
            return jnp.concatenate([ref[b : b + 1, :] for b in blocks], axis=1)

        for tile, slot, pick, put in (
            (src_tile, src_slot, src_pick, src_put),
            (dst_tile, dst_slot, dst_pick, dst_put),
        ):
            index = jnp.concatenate(
                [slot[b : b + 1, :] + (tile[b] - first) * TILE for b in blocks], axis=1
            )
            hit = jnp.where(window == index, 1.0, 0.0)
            put[:, edges] = hit.astype(BF)
            pick[edges, :] = hit.T.astype(BF)
        kind_pick[edges, :] = jnp.where(kind == row(bucket), 1.0, 0.0).T.astype(BF)
        weight = 0.3 * row(envelope) * row(mask).astype(F32)
        scale[edges, :] = jnp.broadcast_to(weight, (C, C)).T


def table_kernel(pick_ref, rows_ref, out):
    row = lax.broadcasted_iota(jnp.int32, (E, 2 * C), 0)
    lane = lax.broadcasted_iota(jnp.int32, (E, 2 * C), 1)
    keep = jnp.where((row % 16) == (lane % 16), 1.0, 0.0).astype(BF)
    for k in range(0, TABLE_STEP, 2):
        pair = jnp.concatenate([rows_ref[k], rows_ref[k + 1]], axis=1)
        value = dot(pick_ref[...], pair).astype(BF) * keep
        out[k] = value[:, :C]
        out[k + 1] = value[:, C:]


def rotation_table(kind_pick, rows, name):
    kinds = kind_pick.shape[1]
    return pl.pallas_call(
        table_kernel,
        grid=(pl.cdiv(NC, TABLE_STEP),),
        in_specs=[
            whole((E, kinds)),
            pl.BlockSpec((TABLE_STEP, kinds, C), lambda i: (i, 0, 0)),
        ],
        out_specs=pl.BlockSpec((TABLE_STEP, E, C), lambda i: (i, 0, 0)),
        out_shape=jax.ShapeDtypeStruct((NC, E, C), BF),
        cost_estimate=pl.CostEstimate(
            flops=NC * E * C * 1024, bytes_accessed=4 * NC * E * C, transcendentals=0
        ),
        name=name,
    )(kind_pick, rows)


def gather_part(ref, rows, part):
    pieces = [ref[coef, rows, :] for coef in part]
    short = 8 - len(part)
    if short:
        pieces.append(jnp.zeros((16 * short, 256), BF))
    return jnp.concatenate(pieces, axis=0)


def turn_part(table_ref, table_rows, ref, rows, part):
    lhs = jnp.concatenate([table_ref[coef, table_rows, :] for coef in part], axis=0)
    return dot(lhs, gather_part(ref, rows, part))


def edge_kernel(
    core_ref,
    table_ref,
    src_ref,
    dst_ref,
    scale_ref,
    low_ref,
    own_ref,
    high_ref,
    w_zero_hbm,
    w_one_hbm,
    w_two_hbm,
    gated_hbm,
    grad_hbm,
    keep_hbm,
    send_hbm,
    both,
    turned,
    rot,
    rot_t,
    grad,
    gated,
    scalar,
    gate_value,
    first,
    total,
    w_zero,
    w_one,
    w_two,
    flat_one,
    flat_two,
    flat_zero,
    joined,
    stage,
    sems,
):
    step = pl.program_id(0)

    def weight_copy(k):
        source, held = ((w_zero_hbm, w_zero), (w_one_hbm, w_one), (w_two_hbm, w_two))[k]
        return pltpu.make_async_copy(source, held, sems.at[k])

    @pl.when(step == 0)
    def _():
        for k in range(3):
            weight_copy(k).start()

    for half, picker in ((0, src_ref), (1, dst_ref)):
        for start, width in COL_PAIRS:
            window = [
                jnp.concatenate(
                    [ref[half * NC + k] for ref in (low_ref, own_ref, high_ref)], axis=0
                )
                for k in range(start, start + width)
            ]
            picked = dot(picker[...], jnp.concatenate(window, axis=1)).astype(BF)
            for k in range(width):
                both[start + k, :, half * C : half * C + C] = picked[:, k * C : (k + 1) * C]

    base = pl.multiple_of(step * CH, CH)

    def turn_group(g, carry):
        rows = pl.ds(pl.multiple_of(g * 16, 16), 16)
        out_rows = pl.ds(pl.multiple_of(base + g * 16, 16), 16)
        for part in PARTS:
            out = turn_part(table_ref, rows, both, rows, part)
            for spot, coef in enumerate(part):
                piece = out[spot * 16 : spot * 16 + 16]
                rot[out_rows, coef * C : (coef + 1) * C] = piece[:, :C].astype(BF)
                turned[coef, rows, :] = piece[:, C:]
        return carry

    lax.fori_loop(0, CH // 16, turn_group, 0, unroll=CH // 16)

    @pl.when(step == 0)
    def _():
        weight_copy(0).wait()

    here = pl.ds(base, CH)
    t = dot(rot[here, : 7 * C], w_zero[:, :C])
    scalar[here, :] = t
    edge_scale = scale_ref[...]
    first[here, :] = turned[0] * edge_scale
    sig = jax.nn.sigmoid(t)
    gate_value[here, :] = sig
    factor = sig * edge_scale
    for coef in range(1, NC):
        grad[here, coef * C : (coef + 1) * C] = (turned[coef] * factor).astype(BF)
    for coef in range(NC):
        rot_t[coef * C : (coef + 1) * C, here] = rot[here, coef * C : (coef + 1) * C].T

    @pl.when(step == STEPS - 1)
    def _():
        weight_copy(1).wait()
        weight_copy(2).wait()
        total[...] = jnp.zeros_like(total)

        def gate(hidden, coef, count, rows):
            sig = gate_value[rows, :]
            for k in range(count):
                value = hidden[:, k * C : (k + 1) * C]
                gated[coef + k, rows, :] = (value * sig).astype(BF)
                if coef + k:
                    lanes = slice((coef + k) * C, (coef + k + 1) * C)
                    total[rows, :] += value * grad[rows, lanes].astype(F32)

        pieces = [slice(k * PIECE, (k + 1) * PIECE) for k in range(E // PIECE)]
        for n in range(4):
            width = 2 if n < 3 else 1
            for rows in pieces:
                gate(
                    dot(rot[rows, : 7 * C], w_zero[:, 2 * n * C : (2 * n + width) * C]),
                    2 * n,
                    width,
                    rows,
                )

        def so_two(weights, begin, half):
            mid = begin + half

            def run(lanes, n, width):
                real, imag = weights[0, :, lanes], weights[1, :, lanes]
                for first, upper, lower in ((begin, real, -imag), (mid, imag, real)):
                    side = jnp.concatenate([upper, lower], axis=0)
                    for rows in pieces:
                        pair = rot[rows, begin * C : (mid + half) * C]
                        gate(dot(pair, side), first + 2 * n, width, rows)

            for n in range(half // 2):
                run(slice(n * 256, (n + 1) * 256), n, 2)
            if half % 2:
                lanes = slice((half - 1) * C, half * C)
                real, imag = weights[0, :, lanes], weights[1, :, lanes]
                upper = jnp.concatenate([real, imag], axis=1)
                lower = jnp.concatenate([-imag, real], axis=1)
                side = jnp.concatenate([upper, lower], axis=0)
                for rows in pieces:
                    value = dot(rot[rows, begin * C : (mid + half) * C], side)
                    gate(value[:, :C], mid - 1, 1, rows)
                    gate(value[:, C:], mid + half - 1, 1, rows)

        so_two(w_one, 7, 6)
        so_two(w_two, 19, 5)

        t_all = scalar[...]
        sig = gate_value[...]
        rest = 1.0 - sig
        grad[:, :C] = (first[...] * sig * (1.0 + t_all * rest) + rest * total[...]).astype(BF)

        outs = [
            pltpu.make_async_copy(gated, gated_hbm, sems.at[3]),
            pltpu.make_async_copy(grad, grad_hbm, sems.at[4]),
        ]
        for copy in outs:
            copy.start()

        core = core_ref[0]

        def spread(value, flat, tile, width, tiles):
            rows = value.shape[0]
            for k in range(width):
                flat[pl.ds(tile + k, rows, stride=tiles), :] = value[:, k * C : (k + 1) * C]

        z_t = rot_t[: 7 * C, :]
        for n in range(4):
            width = 2 if n < 3 else 1
            spread(dot(z_t, grad[:, n * 256 : n * 256 + width * C]), flat_zero, 2 * n, width, 7)

        def complex_grad(begin, half, flat, imaginary):
            mid = begin + half
            plus, minus = rot_t[begin * C : mid * C, :], rot_t[mid * C : (mid + half) * C, :]
            both_t = jnp.concatenate([plus, minus], axis=1)
            for n in range((half + 1) // 2):
                width = min(2, half - 2 * n)
                g_p = grad[:, (begin + 2 * n) * C : (begin + 2 * n + width) * C]
                g_m = grad[:, (mid + 2 * n) * C : (mid + 2 * n + width) * C]
                pair = [g_m, -g_p] if imaginary else [g_p, g_m]
                spread(dot(both_t, jnp.concatenate(pair, axis=0)), flat, 2 * n, width, half)

        def pack(first_chip):
            def body(chip, carry):
                for parity in range(2):
                    device = 2 * chip + parity
                    box = joined.at[lax.rem(device, 8)]
                    box[:72, :] = flat_one[pl.ds(pl.multiple_of(device * ROWS_ONE, 8), 72), :]
                    box[72:128, :] = flat_two[pl.ds(device * ROWS_TWO, 56), :]
                    box[AT_ZERO : AT_ZERO + 56, :] = flat_zero[
                        pl.ds((2 * first_chip + device) * ROWS_ZERO, 56), :
                    ]
                    stage[jnp.bitwise_xor(core, parity), first_chip + chip] = box[
                        :CHUNK, :
                    ].astype(BF)
                return carry

            lax.fori_loop(0, 32, body, 0, unroll=8)

        for imaginary in (False, True):
            chips = pl.ds(32 if imaginary else 0, 32)
            complex_grad(7, 6, flat_one, imaginary)
            complex_grad(19, 5, flat_two, imaginary)
            pack(32 if imaginary else 0)
            for slot, target in ((0, keep_hbm), (1, send_hbm)):
                copy = pltpu.make_async_copy(
                    stage.at[slot, chips], target.at[chips], sems.at[5 + 2 * imaginary + slot]
                )
                copy.start()
                outs.append(copy)
        for copy in outs:
            copy.wait()


def back_kernel(
    table_ref,
    scale_ref,
    src_ref,
    dst_ref,
    w_zero_hbm,
    w_one_hbm,
    w_two_hbm,
    gated_hbm,
    grad_hbm,
    low_hbm,
    own_hbm,
    high_hbm,
    low_ref,
    own_ref,
    high_ref,
    both,
    grad,
    message,
    source,
    w_zero,
    w_one,
    w_two,
    sems,
):
    step = pl.program_id(0)

    @pl.when(step == 0)
    def _():
        copies = []
        for k, (lanes, source, held) in enumerate(
            (
                (slice(0, 7 * C), w_zero_hbm, w_zero),
                (slice(7 * C, 19 * C), w_one_hbm, w_one),
                (slice(19 * C, W), w_two_hbm, w_two),
            )
        ):
            copies.append(
                (
                    pltpu.make_async_copy(source, held, sems.at[2 * k]),
                    pltpu.make_async_copy(
                        grad_hbm.at[:, lanes], grad.at[:, lanes], sems.at[2 * k + 1]
                    ),
                )
            )
        copies.append((pltpu.make_async_copy(gated_hbm, both.at[:, :, :C], sems.at[6]),))
        for group in copies:
            for copy in group:
                copy.start()

        def arrive(k):
            for copy in copies[k]:
                copy.wait()

        arrive(0)

        def put(value, coef, count):
            for k in range(count):
                both[coef + k, :, C:] = value[:, k * C : (k + 1) * C].astype(BF)

        for n in range(4):
            width = 2 if n < 3 else 1
            put(dot_nt(grad[:, : 7 * C], w_zero[2 * n * C : (2 * n + width) * C, :]), 2 * n, width)

        def so_two_back(weights, begin, half):
            mid = begin + half

            def run(rows, n, width):
                pair = grad[:, begin * C : (mid + half) * C]
                real, imag = weights[0, rows, :], weights[1, rows, :]
                put(dot_nt(pair, jnp.concatenate([real, imag], axis=1)), begin + 2 * n, width)
                put(dot_nt(pair, jnp.concatenate([-imag, real], axis=1)), mid + 2 * n, width)

            for n in range(half // 2):
                run(slice(n * 256, (n + 1) * 256), n, 2)
            if half % 2:
                pair = grad[:, begin * C : (mid + half) * C]
                rows = slice((half - 1) * C, half * C)
                real, imag = weights[0, rows, :], weights[1, rows, :]
                upper = jnp.concatenate([real, imag], axis=1)
                lower = jnp.concatenate([-imag, real], axis=1)
                value = dot_nt(pair, jnp.concatenate([upper, lower], axis=0))
                put(value[:, :C], mid - 1, 1)
                put(value[:, C:], mid + half - 1, 1)

        arrive(1)
        so_two_back(w_one, 7, 6)
        arrive(2)
        so_two_back(w_two, 19, 5)
        arrive(3)

    base = pl.multiple_of(step * CH, CH)

    def turn_group(g, carry):
        rows = pl.ds(pl.multiple_of(g * 16, 16), 16)
        out_rows = pl.ds(pl.multiple_of(base + g * 16, 16), 16)
        edge_scale = scale_ref[rows, :]
        for part in PARTS:
            out = turn_part(table_ref, rows, both, out_rows, part)
            for spot, coef in enumerate(part):
                piece = out[spot * 16 : spot * 16 + 16]
                lanes = slice(coef * C, (coef + 1) * C)
                message[out_rows, lanes] = (piece[:, :C] * edge_scale).astype(BF)
                source[out_rows, lanes] = piece[:, C:].astype(BF)
        return carry

    lax.fori_loop(0, CH // 16, turn_group, 0, unroll=CH // 16)

    @pl.when(step == STEPS - 1)
    def _():
        outs = []
        for half, picker, values in ((0, dst_ref, message), (1, src_ref, source)):
            for start, width in COL_PAIRS:
                summed = dot(picker[...], values[:, start * C : (start + width) * C])
                for k in range(width):
                    at = half * NC + start + k
                    piece = summed[:, k * C : (k + 1) * C]
                    low_ref[at] = piece[:TILE].astype(BF)
                    own_ref[at] = piece[TILE : 2 * TILE]
                    high_ref[at] = piece[2 * TILE :].astype(BF)
            kept = slice(half * NC, (half + 1) * NC)
            for k, (held, target) in enumerate(
                ((low_ref, low_hbm), (high_ref, high_hbm), (own_ref, own_hbm))
            ):
                copy = pltpu.make_async_copy(
                    held.at[kept], target.at[kept], sems.at[7 + 3 * half + k]
                )
                copy.start()
                outs.append(copy)
        for copy in outs:
            copy.wait()


def whole(shape):
    return pl.BlockSpec(shape, lambda *_: (0,) * len(shape), pipeline_mode=pl.Buffered(1))


def shift(value, steps):
    count = lax.axis_size("chip") * 2
    pairs = [(i, i + steps) for i in range(count) if 0 <= i + steps < count]
    return lax.ppermute(value, ("chip", "core"), pairs)


def local(
    node_coef,
    cotangent,
    wigner,
    envelope,
    src_tile,
    dst_tile,
    src_slot,
    dst_slot,
    bucket,
    mask,
    w_zero,
    w_one,
    w_two,
):
    core = lax.axis_index("core")
    device = lax.axis_index("chip") * 2 + core
    own = jnp.concatenate(
        [node_coef.transpose(1, 0, 2), cotangent.transpose(1, 0, 2)], axis=0
    )
    low = shift(own, 1)
    high = shift(own, -1)

    kinds = wigner.shape[0]
    smem = pl.BlockSpec(memory_space=pltpu.SMEM)
    vmem = pl.BlockSpec(memory_space=pltpu.VMEM)
    src_pick, dst_pick, src_put, dst_put, kind_pick, scale = pl.pallas_call(
        prepare_kernel,
        in_specs=[smem, smem, smem, vmem, vmem, vmem, vmem, vmem],
        out_specs=[vmem] * 6,
        out_shape=[
            jax.ShapeDtypeStruct((E, 3 * TILE), BF),
            jax.ShapeDtypeStruct((E, 3 * TILE), BF),
            jax.ShapeDtypeStruct((3 * TILE, E), BF),
            jax.ShapeDtypeStruct((3 * TILE, E), BF),
            jax.ShapeDtypeStruct((E, kinds), BF),
            jax.ShapeDtypeStruct((E, C), F32),
        ],
        name="prepare",
    )(
        (device - 1).astype(jnp.int32).reshape(1),
        src_tile,
        dst_tile,
        src_slot,
        dst_slot,
        bucket,
        envelope,
        mask,
    )

    place = place_matrix()
    by_kind = wigner.transpose(1, 2, 0)
    fwd_rows = jnp.einsum("ijb,jl->ibl", by_kind, place, preferred_element_type=F32).astype(BF)
    back_rows = jnp.einsum("ijb,il->jbl", by_kind, place, preferred_element_type=F32).astype(BF)
    fwd_table = rotation_table(kind_pick, fwd_rows, "rotation_table")

    anywhere = pl.BlockSpec(memory_space=pl.ANY)
    halo = whole((2 * NC, TILE, C))
    table_block = pl.BlockSpec((NC, CH, C), lambda s: (0, s, 0))
    scale_block = pl.BlockSpec((CH, C), lambda s: (s, 0))
    weight_scratch = [
        pltpu.VMEM(w_zero.shape, BF),
        pltpu.VMEM(w_one.shape, BF),
        pltpu.VMEM(w_two.shape, BF),
    ]
    gated, grad, keep, send = pl.pallas_call(
        edge_kernel,
        grid=(STEPS,),
        in_specs=[
            pl.BlockSpec(memory_space=pltpu.SMEM),
            table_block,
            pl.BlockSpec((CH, 3 * TILE), lambda s: (s, 0)),
            pl.BlockSpec((CH, 3 * TILE), lambda s: (s, 0)),
            scale_block,
            halo,
            halo,
            halo,
            anywhere,
            anywhere,
            anywhere,
        ],
        out_specs=[anywhere] * 4,
        out_shape=[
            jax.ShapeDtypeStruct((NC, E, C), BF),
            jax.ShapeDtypeStruct((E, W), BF),
            jax.ShapeDtypeStruct((64, CHUNK, C), BF),
            jax.ShapeDtypeStruct((64, CHUNK, C), BF),
        ],
        scratch_shapes=[
            pltpu.VMEM((NC, CH, 2 * C), BF),
            pltpu.VMEM((NC, CH, C), F32),
            pltpu.VMEM((E, W), BF),
            pltpu.VMEM((W, E), BF),
            pltpu.VMEM((E, W), BF),
            pltpu.VMEM((NC, E, C), BF),
            pltpu.VMEM((E, C), F32),
            pltpu.VMEM((E, C), F32),
            pltpu.VMEM((E, C), F32),
            pltpu.VMEM((E, C), F32),
            *weight_scratch,
            pltpu.VMEM((4616, C), F32),
            pltpu.VMEM((3208, C), F32),
            pltpu.VMEM((6280, C), F32),
            pltpu.VMEM((8, 184, C), F32),
            pltpu.VMEM((2, 64, CHUNK, C), BF),
            pltpu.SemaphoreType.DMA((9,)),
        ],
        compiler_params=pltpu.CompilerParams(vmem_limit_bytes=VMEM),
        cost_estimate=pl.CostEstimate(
            flops=20_000_000_000, bytes_accessed=40_000_000, transcendentals=0
        ),
        name="edges_and_weight_grads",
    )(
        core.astype(jnp.int32).reshape(1),
        fwd_table,
        src_pick,
        dst_pick,
        scale,
        low,
        own,
        high,
        w_zero,
        w_one,
        w_two,
    )

    other = lax.ppermute(send, "core", [(0, 1), (1, 0)])
    late_pick, _ = lax.optimization_barrier((kind_pick, send))
    back_table = rotation_table(late_pick, back_rows, "rotation_table_back")
    keep, back_table = lax.optimization_barrier((keep, back_table))
    paired = keep + other
    exchanged = lax.all_to_all(paired, "chip", 0, 0)

    halo_shape = (2 * NC, TILE, C)
    to_low, centre, to_high = pl.pallas_call(
        back_kernel,
        grid=(STEPS,),
        in_specs=[
            table_block,
            scale_block,
            whole((3 * TILE, E)),
            whole((3 * TILE, E)),
            anywhere,
            anywhere,
            anywhere,
            anywhere,
            anywhere,
        ],
        out_specs=[anywhere] * 3,
        out_shape=[
            jax.ShapeDtypeStruct(halo_shape, BF),
            jax.ShapeDtypeStruct(halo_shape, F32),
            jax.ShapeDtypeStruct(halo_shape, BF),
        ],
        scratch_shapes=[
            pltpu.VMEM(halo_shape, BF),
            pltpu.VMEM(halo_shape, F32),
            pltpu.VMEM(halo_shape, BF),
            pltpu.VMEM((NC, E, 2 * C), BF),
            pltpu.VMEM((E, W), BF),
            pltpu.VMEM((E, W), BF),
            pltpu.VMEM((E, W), BF),
            *weight_scratch,
            pltpu.SemaphoreType.DMA((13,)),
        ],
        compiler_params=pltpu.CompilerParams(vmem_limit_bytes=VMEM),
        cost_estimate=pl.CostEstimate(
            flops=20_000_000_000, bytes_accessed=40_000_000, transcendentals=0
        ),
        name="edges_back",
    )(back_table, scale, src_put, dst_put, w_zero, w_one, w_two, gated, grad)

    sums = jnp.sum(exchanged.astype(F32), axis=0)
    grad_one = sums[:ROWS_ONE].reshape(-1)
    grad_two = sums[AT_TWO : AT_TWO + ROWS_TWO].reshape(-1)
    grad_zero = sums[AT_ZERO : AT_ZERO + ROWS_ZERO].reshape(-1)
    from_high, from_low, grad_zero, grad_one, grad_two = lax.optimization_barrier(
        (shift(to_low, -1), shift(to_high, 1), grad_zero, grad_one, grad_two)
    )

    def total(part):
        value = centre[part] + from_high[part].astype(F32) + from_low[part].astype(F32)
        return (own[part].astype(F32) + value).astype(BF).transpose(1, 0, 2)

    updated = total(slice(0, NC))
    grad_coef = total(slice(NC, 2 * NC))
    return (updated, grad_coef, grad_zero, grad_one, grad_two)


def solution(mesh):
    fine = Mesh(mesh.devices.reshape(-1, 2), ("chip", "core"))
    both = ("chip", "core")
    rows3, rows2 = P(both, None, None), P(both, None)
    in_specs = (rows3, rows3, P(), rows2, P(both), P(both), rows2, rows2, rows2, rows2, P(), P(), P())
    out_specs = (rows3, rows3, P(both), P(both), P(both))
    return jax.shard_map(local, mesh=fine, in_specs=in_specs, out_specs=out_specs, check_vma=False)
```

```python
import jax
import jax.numpy as jnp
import numpy as np
from jax import lax
from jax.experimental import pallas as pl
from jax.experimental.pallas import tpu as pltpu
from jax.sharding import Mesh, PartitionSpec as P

BF = jnp.bfloat16
F32 = jnp.float32
NC = 29
C = 128
E = 768
CH = 256
STEPS = E // CH
TILE = 64
W = NC * C
PARTS = (
    (1, 7, 13, 2, 8, 14, 19, 24),
    (0, 3, 9, 15, 20, 25),
    (4, 10, 16, 21, 26),
    (5, 11, 17, 22, 27),
    (6, 12, 18, 23, 28),
)
ROWS_ONE, ROWS_TWO, ROWS_ZERO = 72, 50, 49
AT_TWO, AT_ZERO, CHUNK = 72, 122, 176
TABLE_STEP = 10
PIECE = 256
VMEM = 62 * 1024 * 1024
COL_PAIRS = tuple((k, min(2, NC - k)) for k in range(0, NC, 2))


def dot(a, b):
    return jnp.dot(a, b, preferred_element_type=F32)


def dot_nt(a, b):
    return lax.dot_general(a, b, (((1,), (1,)), ((), ())), preferred_element_type=F32)


def place_matrix():
    place = np.zeros((NC, C), np.float32)
    for part in PARTS:
        for spot, coef in enumerate(part):
            place[coef, spot * 16 : spot * 16 + 16] = 1.0
    return jnp.asarray(place, BF)


def prepare_kernel(
    first_ref,
    src_tile,
    dst_tile,
    src_slot,
    dst_slot,
    bucket,
    envelope,
    mask,
    src_pick,
    dst_pick,
    src_put,
    dst_put,
    kind_pick,
    scale,
):
    first = first_ref[0]
    window = lax.broadcasted_iota(jnp.int32, (3 * TILE, C), 0)
    kind = lax.broadcasted_iota(jnp.int32, (kind_pick.shape[1], C), 0)
    for k in range(E // C):
        blocks = (2 * k, 2 * k + 1)
        edges = slice(k * C, (k + 1) * C)

        def row(ref):
            return jnp.concatenate([ref[b : b + 1, :] for b in blocks], axis=1)

        for tile, slot, pick, put in (
            (src_tile, src_slot, src_pick, src_put),
            (dst_tile, dst_slot, dst_pick, dst_put),
        ):
            index = jnp.concatenate(
                [slot[b : b + 1, :] + (tile[b] - first) * TILE for b in blocks], axis=1
            )
            hit = jnp.where(window == index, 1.0, 0.0)
            put[:, edges] = hit.astype(BF)
            pick[edges, :] = hit.T.astype(BF)
        kind_pick[edges, :] = jnp.where(kind == row(bucket), 1.0, 0.0).T.astype(BF)
        weight = 0.3 * row(envelope) * row(mask).astype(F32)
        scale[edges, :] = jnp.broadcast_to(weight, (C, C)).T


def table_kernel(pick_ref, rows_ref, out):
    row = lax.broadcasted_iota(jnp.int32, (E, 2 * C), 0)
    lane = lax.broadcasted_iota(jnp.int32, (E, 2 * C), 1)
    keep = jnp.where((row % 16) == (lane % 16), 1.0, 0.0).astype(BF)
    for k in range(0, TABLE_STEP, 2):
        pair = jnp.concatenate([rows_ref[k], rows_ref[k + 1]], axis=1)
        value = dot(pick_ref[...], pair).astype(BF) * keep
        out[k] = value[:, :C]
        out[k + 1] = value[:, C:]


def rotation_table(kind_pick, rows, name):
    kinds = kind_pick.shape[1]
    return pl.pallas_call(
        table_kernel,
        grid=(pl.cdiv(NC, TABLE_STEP),),
        in_specs=[
            whole((E, kinds)),
            pl.BlockSpec((TABLE_STEP, kinds, C), lambda i: (i, 0, 0)),
        ],
        out_specs=pl.BlockSpec((TABLE_STEP, E, C), lambda i: (i, 0, 0)),
        out_shape=jax.ShapeDtypeStruct((NC, E, C), BF),
        cost_estimate=pl.CostEstimate(
            flops=NC * E * C * 1024, bytes_accessed=4 * NC * E * C, transcendentals=0
        ),
        name=name,
    )(kind_pick, rows)


def gather_part(ref, rows, part):
    pieces = [ref[coef, rows, :] for coef in part]
    short = 8 - len(part)
    if short:
        pieces.append(jnp.zeros((16 * short, 256), BF))
    return jnp.concatenate(pieces, axis=0)


def turn_part(table_ref, table_rows, ref, rows, part):
    lhs = jnp.concatenate([table_ref[coef, table_rows, :] for coef in part], axis=0)
    return dot(lhs, gather_part(ref, rows, part))


def edge_kernel(
    core_ref,
    table_ref,
    src_ref,
    dst_ref,
    scale_ref,
    low_ref,
    own_ref,
    high_ref,
    w_zero_hbm,
    w_one_hbm,
    w_two_hbm,
    gated_hbm,
    grad_hbm,
    keep_hbm,
    send_hbm,
    both,
    turned,
    rot,
    rot_t,
    grad,
    gated,
    scalar,
    gate_value,
    first,
    total,
    w_zero,
    w_one,
    w_two,
    flat_one,
    flat_two,
    flat_zero,
    joined,
    stage,
    sems,
):
    step = pl.program_id(0)

    def weight_copy(k):
        source, held = ((w_zero_hbm, w_zero), (w_one_hbm, w_one), (w_two_hbm, w_two))[k]
        return pltpu.make_async_copy(source, held, sems.at[k])

    @pl.when(step == 0)
    def _():
        for k in range(3):
            weight_copy(k).start()

    for half, picker in ((0, src_ref), (1, dst_ref)):
        for start, width in COL_PAIRS:
            window = [
                jnp.concatenate(
                    [ref[half * NC + k] for ref in (low_ref, own_ref, high_ref)], axis=0
                )
                for k in range(start, start + width)
            ]
            picked = dot(picker[...], jnp.concatenate(window, axis=1)).astype(BF)
            for k in range(width):
                both[start + k, :, half * C : half * C + C] = picked[:, k * C : (k + 1) * C]

    base = pl.multiple_of(step * CH, CH)

    def turn_group(g, carry):
        rows = pl.ds(pl.multiple_of(g * 16, 16), 16)
        out_rows = pl.ds(pl.multiple_of(base + g * 16, 16), 16)
        for part in PARTS:
            out = turn_part(table_ref, rows, both, rows, part)
            for spot, coef in enumerate(part):
                piece = out[spot * 16 : spot * 16 + 16]
                rot[out_rows, coef * C : (coef + 1) * C] = piece[:, :C].astype(BF)
                turned[coef, rows, :] = piece[:, C:]
        return carry

    lax.fori_loop(0, CH // 16, turn_group, 0, unroll=CH // 16)

    @pl.when(step == 0)
    def _():
        weight_copy(0).wait()

    here = pl.ds(base, CH)
    t = dot(rot[here, : 7 * C], w_zero[:, :C])
    scalar[here, :] = t
    edge_scale = scale_ref[...]
    first[here, :] = turned[0] * edge_scale
    sig = jax.nn.sigmoid(t)
    gate_value[here, :] = sig
    factor = sig * edge_scale
    for coef in range(1, NC):
        grad[here, coef * C : (coef + 1) * C] = (turned[coef] * factor).astype(BF)
    for coef in range(NC):
        rot_t[coef * C : (coef + 1) * C, here] = rot[here, coef * C : (coef + 1) * C].T

    @pl.when(step == STEPS - 1)
    def _():
        weight_copy(1).wait()
        weight_copy(2).wait()
        total[...] = jnp.zeros_like(total)

        def gate(hidden, coef, count, rows):
            sig = gate_value[rows, :]
            for k in range(count):
                value = hidden[:, k * C : (k + 1) * C]
                gated[coef + k, rows, :] = (value * sig).astype(BF)
                if coef + k:
                    lanes = slice((coef + k) * C, (coef + k + 1) * C)
                    total[rows, :] += value * grad[rows, lanes].astype(F32)

        pieces = [slice(k * PIECE, (k + 1) * PIECE) for k in range(E // PIECE)]
        for n in range(4):
            width = 2 if n < 3 else 1
            for rows in pieces:
                gate(
                    dot(rot[rows, : 7 * C], w_zero[:, 2 * n * C : (2 * n + width) * C]),
                    2 * n,
                    width,
                    rows,
                )

        def so_two(weights, begin, half):
            mid = begin + half

            def run(lanes, n, width):
                real, imag = weights[0, :, lanes], weights[1, :, lanes]
                for first, upper, lower in ((begin, real, -imag), (mid, imag, real)):
                    side = jnp.concatenate([upper, lower], axis=0)
                    for rows in pieces:
                        pair = rot[rows, begin * C : (mid + half) * C]
                        gate(dot(pair, side), first + 2 * n, width, rows)

            for n in range(half // 2):
                run(slice(n * 256, (n + 1) * 256), n, 2)
            if half % 2:
                lanes = slice((half - 1) * C, half * C)
                real, imag = weights[0, :, lanes], weights[1, :, lanes]
                upper = jnp.concatenate([real, imag], axis=1)
                lower = jnp.concatenate([-imag, real], axis=1)
                side = jnp.concatenate([upper, lower], axis=0)
                for rows in pieces:
                    value = dot(rot[rows, begin * C : (mid + half) * C], side)
                    gate(value[:, :C], mid - 1, 1, rows)
                    gate(value[:, C:], mid + half - 1, 1, rows)

        so_two(w_one, 7, 6)
        so_two(w_two, 19, 5)

        t_all = scalar[...]
        sig = gate_value[...]
        rest = 1.0 - sig
        grad[:, :C] = (first[...] * sig * (1.0 + t_all * rest) + rest * total[...]).astype(BF)

        outs = [
            pltpu.make_async_copy(gated, gated_hbm, sems.at[3]),
            pltpu.make_async_copy(grad, grad_hbm, sems.at[4]),
        ]
        for copy in outs:
            copy.start()

        core = core_ref[0]

        def spread(value, flat, tile, width, tiles):
            rows = value.shape[0]
            for k in range(width):
                flat[pl.ds(tile + k, rows, stride=tiles), :] = value[:, k * C : (k + 1) * C]

        z_t = rot_t[: 7 * C, :]
        for n in range(4):
            width = 2 if n < 3 else 1
            spread(dot(z_t, grad[:, n * 256 : n * 256 + width * C]), flat_zero, 2 * n, width, 7)

        def complex_grad(begin, half, flat, imaginary):
            mid = begin + half
            plus, minus = rot_t[begin * C : mid * C, :], rot_t[mid * C : (mid + half) * C, :]
            both_t = jnp.concatenate([plus, minus], axis=1)
            for n in range((half + 1) // 2):
                width = min(2, half - 2 * n)
                g_p = grad[:, (begin + 2 * n) * C : (begin + 2 * n + width) * C]
                g_m = grad[:, (mid + 2 * n) * C : (mid + 2 * n + width) * C]
                pair = [g_m, -g_p] if imaginary else [g_p, g_m]
                spread(dot(both_t, jnp.concatenate(pair, axis=0)), flat, 2 * n, width, half)

        def pack(first_chip):
            def body(chip, carry):
                for parity in range(2):
                    device = 2 * chip + parity
                    box = joined.at[lax.rem(device, 8)]
                    box[:72, :] = flat_one[pl.ds(pl.multiple_of(device * ROWS_ONE, 8), 72), :]
                    box[72:128, :] = flat_two[pl.ds(device * ROWS_TWO, 56), :]
                    box[AT_ZERO : AT_ZERO + 56, :] = flat_zero[
                        pl.ds((2 * first_chip + device) * ROWS_ZERO, 56), :
                    ]
                    stage[jnp.bitwise_xor(core, parity), first_chip + chip] = box[
                        :CHUNK, :
                    ].astype(BF)
                return carry

            lax.fori_loop(0, 32, body, 0, unroll=8)

        for imaginary in (False, True):
            chips = pl.ds(32 if imaginary else 0, 32)
            complex_grad(7, 6, flat_one, imaginary)
            complex_grad(19, 5, flat_two, imaginary)
            pack(32 if imaginary else 0)
            for slot, target in ((0, keep_hbm), (1, send_hbm)):
                copy = pltpu.make_async_copy(
                    stage.at[slot, chips], target.at[chips], sems.at[5 + 2 * imaginary + slot]
                )
                copy.start()
                outs.append(copy)
        for copy in outs:
            copy.wait()


def back_kernel(
    table_ref,
    scale_ref,
    src_ref,
    dst_ref,
    w_zero_hbm,
    w_one_hbm,
    w_two_hbm,
    gated_hbm,
    grad_hbm,
    low_hbm,
    own_hbm,
    high_hbm,
    low_ref,
    own_ref,
    high_ref,
    both,
    grad,
    message,
    source,
    w_zero,
    w_one,
    w_two,
    sems,
):
    step = pl.program_id(0)

    @pl.when(step == 0)
    def _():
        copies = []
        for k, (lanes, source, held) in enumerate(
            (
                (slice(0, 7 * C), w_zero_hbm, w_zero),
                (slice(7 * C, 19 * C), w_one_hbm, w_one),
                (slice(19 * C, W), w_two_hbm, w_two),
            )
        ):
            copies.append(
                (
                    pltpu.make_async_copy(source, held, sems.at[2 * k]),
                    pltpu.make_async_copy(
                        grad_hbm.at[:, lanes], grad.at[:, lanes], sems.at[2 * k + 1]
                    ),
                )
            )
        copies.append((pltpu.make_async_copy(gated_hbm, both.at[:, :, :C], sems.at[6]),))
        for group in copies:
            for copy in group:
                copy.start()

        def arrive(k):
            for copy in copies[k]:
                copy.wait()

        arrive(0)

        pieces = [slice(k * PIECE, (k + 1) * PIECE) for k in range(E // PIECE)]

        def put(value, coef, count, rows):
            for k in range(count):
                both[coef + k, rows, C:] = value[:, k * C : (k + 1) * C].astype(BF)

        for n in range(4):
            width = 2 if n < 3 else 1
            side = w_zero[2 * n * C : (2 * n + width) * C, :]
            for rows in pieces:
                put(dot_nt(grad[rows, : 7 * C], side), 2 * n, width, rows)

        def so_two_back(weights, begin, half):
            mid = begin + half

            lanes = slice(begin * C, (mid + half) * C)

            def run(tile, n, width):
                real, imag = weights[0, tile, :], weights[1, tile, :]
                for first, left, right in ((begin, real, imag), (mid, -imag, real)):
                    side = jnp.concatenate([left, right], axis=1)
                    for rows in pieces:
                        put(dot_nt(grad[rows, lanes], side), first + 2 * n, width, rows)

            for n in range(half // 2):
                run(slice(n * 256, (n + 1) * 256), n, 2)
            if half % 2:
                tile = slice((half - 1) * C, half * C)
                real, imag = weights[0, tile, :], weights[1, tile, :]
                upper = jnp.concatenate([real, imag], axis=1)
                lower = jnp.concatenate([-imag, real], axis=1)
                side = jnp.concatenate([upper, lower], axis=0)
                for rows in pieces:
                    value = dot_nt(grad[rows, lanes], side)
                    put(value[:, :C], mid - 1, 1, rows)
                    put(value[:, C:], mid + half - 1, 1, rows)

        arrive(1)
        so_two_back(w_one, 7, 6)
        arrive(2)
        so_two_back(w_two, 19, 5)
        arrive(3)

    base = pl.multiple_of(step * CH, CH)

    def turn_group(g, carry):
        rows = pl.ds(pl.multiple_of(g * 16, 16), 16)
        out_rows = pl.ds(pl.multiple_of(base + g * 16, 16), 16)
        edge_scale = scale_ref[rows, :]
        for part in PARTS:
            out = turn_part(table_ref, rows, both, out_rows, part)
            for spot, coef in enumerate(part):
                piece = out[spot * 16 : spot * 16 + 16]
                lanes = slice(coef * C, (coef + 1) * C)
                message[out_rows, lanes] = (piece[:, :C] * edge_scale).astype(BF)
                source[out_rows, lanes] = piece[:, C:].astype(BF)
        return carry

    lax.fori_loop(0, CH // 16, turn_group, 0, unroll=CH // 16)

    @pl.when(step == STEPS - 1)
    def _():
        outs = []
        for half, picker, values in ((0, dst_ref, message), (1, src_ref, source)):
            for start, width in COL_PAIRS:
                summed = dot(picker[...], values[:, start * C : (start + width) * C])
                for k in range(width):
                    at = half * NC + start + k
                    piece = summed[:, k * C : (k + 1) * C]
                    low_ref[at] = piece[:TILE].astype(BF)
                    own_ref[at] = piece[TILE : 2 * TILE]
                    high_ref[at] = piece[2 * TILE :].astype(BF)
            kept = slice(half * NC, (half + 1) * NC)
            for k, (held, target) in enumerate(
                ((low_ref, low_hbm), (high_ref, high_hbm), (own_ref, own_hbm))
            ):
                copy = pltpu.make_async_copy(
                    held.at[kept], target.at[kept], sems.at[7 + 3 * half + k]
                )
                copy.start()
                outs.append(copy)
        for copy in outs:
            copy.wait()


def whole(shape):
    return pl.BlockSpec(shape, lambda *_: (0,) * len(shape), pipeline_mode=pl.Buffered(1))


def shift(value, steps):
    count = lax.axis_size("chip") * 2
    pairs = [(i, i + steps) for i in range(count) if 0 <= i + steps < count]
    return lax.ppermute(value, ("chip", "core"), pairs)


def local(
    node_coef,
    cotangent,
    wigner,
    envelope,
    src_tile,
    dst_tile,
    src_slot,
    dst_slot,
    bucket,
    mask,
    w_zero,
    w_one,
    w_two,
):
    core = lax.axis_index("core")
    device = lax.axis_index("chip") * 2 + core
    own = jnp.concatenate(
        [node_coef.transpose(1, 0, 2), cotangent.transpose(1, 0, 2)], axis=0
    )
    low = shift(own, 1)
    high = shift(own, -1)

    kinds = wigner.shape[0]
    smem = pl.BlockSpec(memory_space=pltpu.SMEM)
    vmem = pl.BlockSpec(memory_space=pltpu.VMEM)
    src_pick, dst_pick, src_put, dst_put, kind_pick, scale = pl.pallas_call(
        prepare_kernel,
        in_specs=[smem, smem, smem, vmem, vmem, vmem, vmem, vmem],
        out_specs=[vmem] * 6,
        out_shape=[
            jax.ShapeDtypeStruct((E, 3 * TILE), BF),
            jax.ShapeDtypeStruct((E, 3 * TILE), BF),
            jax.ShapeDtypeStruct((3 * TILE, E), BF),
            jax.ShapeDtypeStruct((3 * TILE, E), BF),
            jax.ShapeDtypeStruct((E, kinds), BF),
            jax.ShapeDtypeStruct((E, C), F32),
        ],
        name="prepare",
    )(
        (device - 1).astype(jnp.int32).reshape(1),
        src_tile,
        dst_tile,
        src_slot,
        dst_slot,
        bucket,
        envelope,
        mask,
    )

    place = place_matrix()
    by_kind = wigner.transpose(1, 2, 0)
    fwd_rows = jnp.einsum("ijb,jl->ibl", by_kind, place, preferred_element_type=F32).astype(BF)
    back_rows = jnp.einsum("ijb,il->jbl", by_kind, place, preferred_element_type=F32).astype(BF)
    fwd_table = rotation_table(kind_pick, fwd_rows, "rotation_table")

    anywhere = pl.BlockSpec(memory_space=pl.ANY)
    halo = whole((2 * NC, TILE, C))
    table_block = pl.BlockSpec((NC, CH, C), lambda s: (0, s, 0))
    scale_block = pl.BlockSpec((CH, C), lambda s: (s, 0))
    weight_scratch = [
        pltpu.VMEM(w_zero.shape, BF),
        pltpu.VMEM(w_one.shape, BF),
        pltpu.VMEM(w_two.shape, BF),
    ]
    gated, grad, keep, send = pl.pallas_call(
        edge_kernel,
        grid=(STEPS,),
        in_specs=[
            pl.BlockSpec(memory_space=pltpu.SMEM),
            table_block,
            pl.BlockSpec((CH, 3 * TILE), lambda s: (s, 0)),
            pl.BlockSpec((CH, 3 * TILE), lambda s: (s, 0)),
            scale_block,
            halo,
            halo,
            halo,
            anywhere,
            anywhere,
            anywhere,
        ],
        out_specs=[anywhere] * 4,
        out_shape=[
            jax.ShapeDtypeStruct((NC, E, C), BF),
            jax.ShapeDtypeStruct((E, W), BF),
            jax.ShapeDtypeStruct((64, CHUNK, C), BF),
            jax.ShapeDtypeStruct((64, CHUNK, C), BF),
        ],
        scratch_shapes=[
            pltpu.VMEM((NC, CH, 2 * C), BF),
            pltpu.VMEM((NC, CH, C), F32),
            pltpu.VMEM((E, W), BF),
            pltpu.VMEM((W, E), BF),
            pltpu.VMEM((E, W), BF),
            pltpu.VMEM((NC, E, C), BF),
            pltpu.VMEM((E, C), F32),
            pltpu.VMEM((E, C), F32),
            pltpu.VMEM((E, C), F32),
            pltpu.VMEM((E, C), F32),
            *weight_scratch,
            pltpu.VMEM((4616, C), F32),
            pltpu.VMEM((3208, C), F32),
            pltpu.VMEM((6280, C), F32),
            pltpu.VMEM((8, 184, C), F32),
            pltpu.VMEM((2, 64, CHUNK, C), BF),
            pltpu.SemaphoreType.DMA((9,)),
        ],
        compiler_params=pltpu.CompilerParams(vmem_limit_bytes=VMEM),
        cost_estimate=pl.CostEstimate(
            flops=20_000_000_000, bytes_accessed=40_000_000, transcendentals=0
        ),
        name="edges_and_weight_grads",
    )(
        core.astype(jnp.int32).reshape(1),
        fwd_table,
        src_pick,
        dst_pick,
        scale,
        low,
        own,
        high,
        w_zero,
        w_one,
        w_two,
    )

    other = lax.ppermute(send, "core", [(0, 1), (1, 0)])
    late_pick, _ = lax.optimization_barrier((kind_pick, send))
    back_table = rotation_table(late_pick, back_rows, "rotation_table_back")
    keep, back_table = lax.optimization_barrier((keep, back_table))
    paired = keep + other
    exchanged = lax.all_to_all(paired, "chip", 0, 0)

    halo_shape = (2 * NC, TILE, C)
    to_low, centre, to_high = pl.pallas_call(
        back_kernel,
        grid=(STEPS,),
        in_specs=[
            table_block,
            scale_block,
            whole((3 * TILE, E)),
            whole((3 * TILE, E)),
            anywhere,
            anywhere,
            anywhere,
            anywhere,
            anywhere,
        ],
        out_specs=[anywhere] * 3,
        out_shape=[
            jax.ShapeDtypeStruct(halo_shape, BF),
            jax.ShapeDtypeStruct(halo_shape, F32),
            jax.ShapeDtypeStruct(halo_shape, BF),
        ],
        scratch_shapes=[
            pltpu.VMEM(halo_shape, BF),
            pltpu.VMEM(halo_shape, F32),
            pltpu.VMEM(halo_shape, BF),
            pltpu.VMEM((NC, E, 2 * C), BF),
            pltpu.VMEM((E, W), BF),
            pltpu.VMEM((E, W), BF),
            pltpu.VMEM((E, W), BF),
            *weight_scratch,
            pltpu.SemaphoreType.DMA((13,)),
        ],
        compiler_params=pltpu.CompilerParams(vmem_limit_bytes=VMEM),
        cost_estimate=pl.CostEstimate(
            flops=20_000_000_000, bytes_accessed=40_000_000, transcendentals=0
        ),
        name="edges_back",
    )(back_table, scale, src_put, dst_put, w_zero, w_one, w_two, gated, grad)

    sums = jnp.sum(exchanged.astype(F32), axis=0)
    grad_one = sums[:ROWS_ONE].reshape(-1)
    grad_two = sums[AT_TWO : AT_TWO + ROWS_TWO].reshape(-1)
    grad_zero = sums[AT_ZERO : AT_ZERO + ROWS_ZERO].reshape(-1)
    from_high, from_low, grad_zero, grad_one, grad_two = lax.optimization_barrier(
        (shift(to_low, -1), shift(to_high, 1), grad_zero, grad_one, grad_two)
    )

    def total(part):
        value = centre[part] + from_high[part].astype(F32) + from_low[part].astype(F32)
        return (own[part].astype(F32) + value).astype(BF).transpose(1, 0, 2)

    updated = total(slice(0, NC))
    grad_coef = total(slice(NC, 2 * NC))
    return (updated, grad_coef, grad_zero, grad_one, grad_two)


def solution(mesh):
    fine = Mesh(mesh.devices.reshape(-1, 2), ("chip", "core"))
    both = ("chip", "core")
    rows3, rows2 = P(both, None, None), P(both, None)
    in_specs = (rows3, rows3, P(), rows2, P(both), P(both), rows2, rows2, rows2, rows2, P(), P(), P())
    out_specs = (rows3, rows3, P(both), P(both), P(both))
    return jax.shard_map(local, mesh=fine, in_specs=in_specs, out_specs=out_specs, check_vma=False)
```
